512 devices in a mesh: grp: 16 (over x, y), row: 32 (over z, core).
Axes of the slice: x: 4, y: 4, z: 16, core: 2. Of those that a mesh axis runs over, the one named last changes fastest.
Arguments:
- start_vectors: float32 [64, 524288], P(None, ('grp', 'row'))
- start_directions: float32 [64, 524288], P(None, ('grp', 'row'))
- tiles: bfloat16 [53248, 128, 128], P(('grp', 'row')), may hold values from -0.109375 to 0.109375
- tile_row: int32 [53248], P(('grp', 'row')), may hold values from 0 to 7, as said below
- tile_slot: int32 [53248], P(('grp', 'row')), may hold values from 0 to 103, as said below
- tile_count: int32 [512], P(('grp', 'row')), may hold values from 8 to 100, as said below
- send_row: int32 [32768], P(('grp', 'row')), may hold values from -1 to 7, as said below
- send_grp: int32 [16384], P(('grp', 'row')), may hold values from -1 to 7, as said below
- ritz: float32 [2, 192, 128], replicated, may hold values from -0.4375 to 0.4375
Outputs:
- final_vectors: float32 [64, 524288], P(None, ('grp', 'row'))
- final_directions: float32 [64, 524288], P(None, ('grp', 'row'))
The draws below stay inside these ranges and needn't reach their ends.
Inputs may be any that keep to these rules, and one draw needn't show every extreme that they name: `tile_row`: own row block that a tile slot adds into. `tile_slot`: index into device d's block table: 8 own row blocks, then 32 * 2 slots from its community (p * 2 + s from row index p), then 16 * 2 slots from other communities (h * 2 + s from community h). Among a device's live tile slots each own block and each filled slot is named exactly once, and no empty slot. A device's live tile slots are its first tile_count entries; the rest are unused. In each community one device has every slot from other devices filled. `send_row`: entry (d * 32 + r) * 2 + s: the own row block that device d sends in slot s to the device of row index r in its community, or -1 for an empty slot. A sender's filled entries to one receiver are distinct and come first; its entries to itself are -1; in each community one device receives all 2 slots from every other member. `send_grp`: entry (d * 16 + h) * 2 + s: the own row block that device d sends in slot s to the device of the same row index in community h, or -1 for an empty slot. Filled entries to one receiver are distinct and come first; entries to its own community are -1; the device that receives all in-community slots also receives all 2 slots from every other community.
All inputs are finite; a program needn't handle non-finite values.
Results may differ from the reference program's by a relative error of at most 0.0032.
Values may be sent and summed in bfloat16 or wider, within the bound.
A program may use at most 64 MiB of HBM per device.

```python
import math
import jax
import jax.numpy as jnp
from jax import lax

K = 64
BS = 128
RB = 8
HR = 2
HG = 2
ITERS = 2
TILES = 104
ROWS = 524288
N_GRP = 16
N_ROW = 32


def pick_distinct(key, shape, count):
    scores = jax.random.randint(key, shape + (RB,), 0, 2 ** 20) * RB + jnp.arange(RB, dtype=jnp.int32)
    return jnp.argsort(scores, axis=-1)[..., :count].astype(jnp.int32)


def slot_counts(key, shape, capacity):
    raw_counts = jax.random.randint(key, shape, 0, capacity + 2)
    return jnp.clip(raw_counts - 1, 0, capacity)


def graph_tables(key):
    subkeys = jax.random.split(key, 7)
    device_total = N_GRP * N_ROW
    busiest = jax.random.randint(subkeys[0], (N_GRP,), 0, N_ROW)
    sender_ids = jnp.arange(N_ROW)[None, :, None]
    receiver_ids = jnp.arange(N_ROW)[None, None, :]
    near_counts = slot_counts(subkeys[1], (N_GRP, N_ROW, N_ROW), HR)
    near_counts = jnp.where(receiver_ids == busiest[:, None, None], HR, near_counts)
    near_counts = jnp.where(sender_ids == receiver_ids, 0, near_counts)
    near_blocks = pick_distinct(subkeys[2], (N_GRP, N_ROW, N_ROW), HR)
    near_slots = jnp.arange(HR)[None, None, None, :]
    near_send = jnp.where(near_slots < near_counts[..., None], near_blocks, -1).astype(jnp.int32)
    from_ids = jnp.arange(N_GRP)[:, None, None]
    to_ids = jnp.arange(N_GRP)[None, None, :]
    row_ids = jnp.arange(N_ROW)[None, :, None]
    far_counts = slot_counts(subkeys[3], (N_GRP, N_ROW, N_GRP), HG)
    far_counts = jnp.where(row_ids == busiest[None, None, :], HG, far_counts)
    far_counts = jnp.where(from_ids == to_ids, 0, far_counts)
    far_blocks = pick_distinct(subkeys[4], (N_GRP, N_ROW, N_GRP), HG)
    far_slots = jnp.arange(HG)[None, None, None, :]
    far_send = jnp.where(far_slots < far_counts[..., None], far_blocks, -1).astype(jnp.int32)
    near_live = near_slots < near_counts.transpose(0, 2, 1)[..., None]
    far_live = far_slots < far_counts.transpose(2, 1, 0)[..., None]
    live = jnp.concatenate([jnp.ones((device_total, RB), bool), near_live.reshape(device_total, N_ROW * HR), far_live.reshape(device_total, N_GRP * HG)], axis=1)
    candidate_rows = jnp.concatenate([jnp.broadcast_to(jnp.arange(RB, dtype=jnp.int32)[None, :], (device_total, RB)), jax.random.randint(subkeys[5], (device_total, TILES - RB), 0, RB)], axis=1)
    scores = jax.random.randint(subkeys[6], (device_total, TILES), 0, 2 ** 20) * TILES + jnp.arange(TILES, dtype=jnp.int32)
    scores = jnp.where(live, scores, scores + 2 ** 28)
    order = jnp.argsort(scores, axis=1).astype(jnp.int32)
    tile_rows = jnp.take_along_axis(candidate_rows, order, axis=1).astype(jnp.int32)
    counts = jnp.sum(live.astype(jnp.int32), axis=1).astype(jnp.int32)
    return (tile_rows.reshape(-1), order.reshape(-1), counts, near_send.reshape(-1), far_send.reshape(-1))


def draw_tile_row(key, part):
    tables = graph_tables(key)
    return tables[0]


def draw_tile_slot(key, part):
    tables = graph_tables(key)
    return tables[1]


def draw_tile_count(key, part):
    tables = graph_tables(key)
    return tables[2]


def draw_send_row(key, part):
    tables = graph_tables(key)
    return tables[3]


def draw_send_grp(key, part):
    tables = graph_tables(key)
    return tables[4]


def rising_field(key, ramp_rise, noise_span):
    first, second, third = jax.random.split(key, 3)
    noise = jax.random.normal(first, (K, ROWS), jnp.float32)
    position = jnp.arange(ROWS, dtype=jnp.float32)[None, :] / ROWS
    ramp = jnp.exp(math.log(ramp_rise) * position)
    row_scale = jnp.exp(jax.random.uniform(second, (1, ROWS), jnp.float32, 0.0, math.log(noise_span)))
    column_scale = jnp.exp(jax.random.uniform(third, (K, 1), jnp.float32, 0.0, math.log(noise_span)))
    return (noise * ramp * row_scale * column_scale / 6.0).astype(jnp.float32)


def draw_start_vectors(key, part):
    key = jax.random.fold_in(key, 5)
    return rising_field(key, 4.0, 10.0)


def draw_start_directions(key, part):
    key = jax.random.fold_in(key, 6)
    return rising_field(key, 4.0, 8.0)


def shard_levels(rng, extent, cuts, least, high):
    level, own = 1.0, jax.random.fold_in(rng, 6)
    for axis_at, parts in cuts:
        heights = jnp.exp(jax.random.uniform(jax.random.fold_in(own, axis_at), (parts,), jnp.float32, least / len(cuts), high / len(cuts)))
        level = level * jnp.repeat(heights, extent[axis_at] // parts).reshape([-1 if axis == axis_at else 1 for axis in range(len(extent))])
    return level


def normal_values(own_key, extent, deviation, reach, cuts=(), kind=jnp.bfloat16):
    level = shard_levels(own_key, extent, cuts, -0.22, 0.18) if cuts else 1.0
    array = jax.random.normal(own_key, extent, jnp.float32) * deviation * level
    return jnp.minimum(jnp.maximum(array, -reach), reach).astype(kind)


def setup_inputs(seed: int = 0) -> dict:
    splits = jax.random.split(jax.random.key(seed), 10)
    return {
        "start_vectors": draw_start_vectors(jax.random.fold_in(splits[9], 71), 0),
        "start_directions": draw_start_directions(jax.random.fold_in(splits[9], 71), 0),
        "tiles": normal_values(splits[2], (TILES * N_GRP * N_ROW, BS, BS), (24 * BS) ** -0.5, 0.109375, ((0, 512),)),
        "tile_row": draw_tile_row(jax.random.fold_in(splits[9], 71), 0),
        "tile_slot": draw_tile_slot(jax.random.fold_in(splits[9], 71), 0),
        "tile_count": draw_tile_count(jax.random.fold_in(splits[9], 71), 0),
        "send_row": draw_send_row(jax.random.fold_in(splits[9], 71), 0),
        "send_grp": draw_send_grp(jax.random.fold_in(splits[9], 71), 0),
        "ritz": normal_values(splits[8], (ITERS, 3 * K, 2 * K), (3 * K) ** -0.5, 0.4375, (), jnp.float32),
    }


def source_table(send_row, send_grp):
    device_total = N_GRP * N_ROW
    empty_block = N_GRP * N_ROW * RB
    device_ids = jnp.arange(device_total, dtype=jnp.int32)
    own_ids = device_ids[:, None] * RB + jnp.arange(RB, dtype=jnp.int32)[None, :]
    near_lists = send_row.reshape(N_GRP, N_ROW, N_ROW, HR).transpose(0, 2, 1, 3)
    group_ids = jnp.arange(N_GRP, dtype=jnp.int32)[:, None, None, None]
    peer_ids = jnp.arange(N_ROW, dtype=jnp.int32)[None, None, :, None]
    near_source = jnp.where(near_lists >= 0, (group_ids * N_ROW + peer_ids) * RB + near_lists, empty_block)
    far_lists = send_grp.reshape(N_GRP, N_ROW, N_GRP, HG).transpose(2, 1, 0, 3)
    row_ids = jnp.arange(N_ROW, dtype=jnp.int32)[None, :, None, None]
    other_ids = jnp.arange(N_GRP, dtype=jnp.int32)[None, None, :, None]
    far_source = jnp.where(far_lists >= 0, (other_ids * N_ROW + row_ids) * RB + far_lists, empty_block)
    return jnp.concatenate([own_ids, near_source.reshape(device_total, N_ROW * HR), far_source.reshape(device_total, N_GRP * HG)], axis=1).astype(jnp.int32)

def tile_terms(padded, tiles, tile_row, tile_slot, tile_count, table):
    targets = jnp.arange(RB, dtype=jnp.int32)
    positions = jnp.arange(TILES, dtype=jnp.int32)

    def one_device(device):
        first = device * TILES
        slots = lax.dynamic_slice_in_dim(tile_slot, first, TILES)
        rows_of = lax.dynamic_slice_in_dim(tile_row, first, TILES)
        values = lax.dynamic_slice_in_dim(tiles, first, TILES, 0).astype(jnp.float32)
        sources = lax.dynamic_index_in_dim(table, device, 0, keepdims=False)[slots]
        picked = jnp.take(padded, sources, axis=1).astype(jnp.float32)
        products = jnp.einsum('ktc,tbc->tkb', picked, values, precision=lax.Precision.HIGHEST)
        active = positions < lax.dynamic_index_in_dim(tile_count, device, 0, keepdims=False)
        onehot = jnp.where(active[:, None] & (rows_of[:, None] == targets[None, :]), 1.0, 0.0).astype(jnp.float32)
        return jnp.einsum('tr,tkb->krb', onehot, products, precision=lax.Precision.HIGHEST)
    pieces = lax.map(one_device, jnp.arange(N_GRP * N_ROW, dtype=jnp.int32))
    return pieces.transpose(1, 0, 2, 3).reshape(K, ROWS)

def reference(start_vectors, start_directions, tiles, tile_row, tile_slot, tile_count, send_row, send_grp, ritz):
    table = source_table(send_row, send_grp)
    vectors, directions = (start_vectors, start_directions)
    for iteration in range(ITERS):
        rounded = vectors.astype(jnp.bfloat16)
        padded = jnp.concatenate([rounded.reshape(K, N_GRP * N_ROW * RB, BS), jnp.zeros((K, 1, BS), jnp.bfloat16)], axis=1)
        affinity = tile_terms(padded, tiles, tile_row, tile_slot, tile_count, table)
        stacked = jnp.concatenate([vectors, affinity, directions], axis=0)
        gram_matrix = jnp.dot(stacked, stacked.T, precision=lax.Precision.HIGHEST) / ROWS
        factor = jnp.linalg.cholesky(gram_matrix)
        coeffs = lax.linalg.triangular_solve(factor, ritz[iteration], left_side=True, lower=True, transpose_a=True)
        update = jnp.dot(coeffs.T, stacked, precision=lax.Precision.HIGHEST)
        vectors, directions = (update[:K], update[K:])
    return (vectors, directions)
```

```python
import functools

import jax
import jax.numpy as jnp
from jax import lax
from jax.experimental import pallas as pl
from jax.experimental.pallas import tpu as pltpu
from jax.sharding import PartitionSpec as P

ITERS = 2
K = 64
BS = 128
RB = 8
NCH = 2
BPC = RB // NCH
UNROLL = 8
F32, BF16, I32 = jnp.float32, jnp.bfloat16, jnp.int32
MESH = pl.DeviceIdType.MESH
HIGH = lax.Precision.HIGHEST


def dot32(a, b, ca, cb):
    return lax.dot_general(
        a, b, (((ca,), (cb,)), ((), ())), precision=HIGH, preferred_element_type=F32
    )


def dot16(a, b, ca, cb):
    return lax.dot_general(a, b, (((ca,), (cb,)), ((), ())), preferred_element_type=F32)


def split(x):
    hi = x.astype(BF16)
    return hi, (x - hi.astype(F32)).astype(BF16)


def dot3(ah, al, bh, bl, ca, cb):
    return dot16(ah, bh, ca, cb) + (dot16(ah, bl, ca, cb) + dot16(al, bh, ca, cb))


class Eliminate:
    def __init__(self, s, work):
        row = lax.broadcasted_iota(I32, (K, K), 0)
        col = lax.broadcasted_iota(I32, (K, K), 1)
        work[:, 0:K] = s
        work[:, K : 2 * K] = jnp.where(row == col, 1.0, 0.0).astype(F32)
        self.rows = [work[8 * i : 8 * i + 8, :] for i in range(K // 8)]
        self.sub = lax.broadcasted_iota(I32, (8, 2 * K), 0)

    def panel(self, p):
        rows, sub = self.rows, self.sub
        wide = (8, 2 * K)
        cols = [
            [
                jnp.broadcast_to(rows[i][:, 8 * p + k : 8 * p + k + 1], wide)
                for i in range(p, K // 8)
            ]
            for k in range(8)
        ]
        for k in range(8):
            inv = lax.rsqrt(jnp.broadcast_to(cols[k][0][k : k + 1, :], wide))
            low = [c * inv for c in cols[k]]
            for j in range(k + 1, 8):
                mult = jnp.broadcast_to(low[0][j : j + 1, :], wide)
                cols[j] = [c - x * mult for c, x in zip(cols[j], low)]
            pivot = jnp.broadcast_to(rows[p][k : k + 1, :], wide) * inv
            below = jnp.where(sub > k, low[0], 0.0)
            rows[p] = jnp.where(sub == k, pivot, rows[p] - below * pivot)
            for i in range(p + 1, K // 8):
                rows[i] = rows[i] - low[i - p] * pivot

    def inverse(self):
        return jnp.concatenate([r[:, K : 2 * K] for r in self.rows], axis=0)


def kernel(
    ng, nz, total_rows, slots,
    sv, sd, tiles, meta, count, send_row, send_grp, ritz,
    out_v, out_d,
    blk, pack, own, tl, runs, sh, sl, iv, ov, sm_iv, sm_ix, mytb, tb, tv, sm_tv,
    pay, rsb, zb, res, work,
    loc_sem, ring_s, ring_r, sib_s, sib_r, far_s, far_r, tb_s, tb_r, tbx_s, tbx_r,
    rs_s, rs_r, z_s, z_r, ag_s, ag_r,
):
    hops = nz // 2
    far0 = 2 * nz * RB
    pieces = 12 if ng >= 12 else 3
    prow = 96 // pieces
    g, r = lax.axis_index("grp"), lax.axis_index("row")
    z, c = r // 2, r % 2
    m = g * 2 + c
    sib = (g, z * 2 + (1 - c))

    def remote(src, dst, ss, rs, dev):
        return pltpu.make_async_remote_copy(
            src_ref=src, dst_ref=dst, send_sem=ss, recv_sem=rs, device_id=dev, device_id_type=MESH
        )

    def loop(n, body):
        def step(i, carry):
            body(i)
            return carry

        lax.fori_loop(0, n, step, 0)

    def plane_dev(i):
        return (i // 2, z * 2 + i % 2)

    barrier = pltpu.get_barrier_semaphore()

    def greet_z(i):
        @pl.when(i != z)
        def _():
            pl.semaphore_signal(barrier, inc=1, device_id=(g, i * 2 + c), device_id_type=MESH)

    def greet_plane(i):
        @pl.when(i != m)
        def _():
            pl.semaphore_signal(barrier, inc=1, device_id=plane_dev(i), device_id_type=MESH)

    loop(nz, greet_z)
    loop(2 * ng, greet_plane)

    tile_load = pltpu.make_async_copy(tiles, tl, loc_sem.at[0])
    tile_load.start()

    def put_vectors(it):
        for b in range(RB):
            x = sh[0:K, b * BS : (b + 1) * BS]
            own[b] = x
            blk[it, r * RB + b] = x

        def fill(h):
            for s in range(2):
                q = jnp.clip(send_grp[h * 2 + s], 0, RB - 1)
                pack[it, h * 2 + s] = own[q]

        loop(ng, fill)
        zero = jnp.zeros((K, BS), BF16)
        blk[it, far0 + 2 * g] = zero
        blk[it, far0 + 2 * g + 1] = zero

    def split_into(row0, x):
        hi, lo = split(x)
        sh[row0 : row0 + K, :] = hi
        sl[row0 : row0 + K, :] = lo

    split_into(0, sv[...])
    split_into(K, sd[...])
    put_vectors(0)
    mytb[...] = jnp.zeros((8, 128), I32)
    mytb[0:1, 0 : 4 * nz] = send_row[...]
    tb[c, z] = mytb[...]

    pl.semaphore_wait(barrier, nz - 1 + 2 * ng - 1)

    def chunk(it, src_z, core, j, n=BPC):
        return blk.at[it, pl.ds((src_z * 2 + core) * RB + j * BPC, n)]

    def ring_src(d, hop):
        return lax.rem(z + nz - (hop - 1), nz) if d == 0 else lax.rem(z + hop - 1, nz)

    def ring_copy(it, d, hop, j):
        ref = chunk(it, ring_src(d, hop), c, j)
        to = lax.rem(z + 1, nz) if d == 0 else lax.rem(z + nz - 1, nz)
        return remote(ref, ref, ring_s.at[it, d, hop - 1, j], ring_r.at[it, d, hop - 1, j], (g, to * 2 + c))

    def ring_here(it, d, hop, j):
        ref = chunk(it, ring_src(d, hop + 1), c, j)
        return remote(ref, ref, ring_s.at[it, d, hop - 1, j], ring_r.at[it, d, hop - 1, j], sib)

    def sib_copy(it, d, hop, j):
        ref = chunk(it, ring_src(d, hop + 1), c, j)
        return remote(ref, ref, sib_s.at[it, d, hop, j], sib_r.at[it, d, hop, j], sib)

    def sib_here(it, d, hop, j):
        ref = chunk(it, ring_src(d, hop + 1), 1 - c, j)
        return remote(ref, ref, sib_s.at[it, d, hop, j], sib_r.at[it, d, hop, j], sib)

    def ring_parts(hop):
        return [
            (d, j)
            for j in range(NCH)
            for d in range(2)
            if hop < hops or (j < NCH // 2) == (d == 0)
        ]

    def own_to_sib(it, core):
        ref = chunk(it, z, core, 0, RB)
        return remote(ref, ref, sib_s.at[it, 0, 0, 0], sib_r.at[it, 0, 0, 0], sib)

    def far_copy(it, h):
        return remote(
            pack.at[it, pl.ds(h * 2, 2)], blk.at[it, pl.ds(far0 + 2 * g, 2)],
            far_s.at[it, h], far_r.at[it, g], (h, r),
        )

    def far_here(it, h):
        return remote(
            pack.at[it, pl.ds(h * 2, 2)], blk.at[it, pl.ds(far0 + 2 * h, 2)],
            far_s.at[it, h], far_r.at[it, h], (h, r),
        )

    def start_exchange(it):
        for d, j in ring_parts(1):
            ring_copy(it, d, 1, j).start()
        own_to_sib(it, c).start()

        def far(h):
            @pl.when(h != g)
            def _():
                far_copy(it, h).start()

        loop(ng, far)

    def ring_step(it, hop):
        for d, j in ring_parts(hop):
            ring_here(it, d, hop, j).wait_recv()
            if hop < hops and (d, j) in ring_parts(hop + 1):
                ring_copy(it, d, hop + 1, j).start()
            sib_copy(it, d, hop, j).start()

    def finish_exchange(it):
        own_to_sib(it, 1 - c).wait_recv()
        for hop in range(1, hops + 1):
            for d, j in ring_parts(hop):
                sib_here(it, d, hop, j).wait_recv()

        def far(h):
            @pl.when(h != g)
            def _():
                far_here(it, h).wait_recv()

        loop(ng, far)

    def drain_exchange(it):
        own_to_sib(it, c).wait_send()
        for hop in range(1, hops + 1):
            for d, j in ring_parts(hop):
                ring_copy(it, d, hop, j).wait_send()
                sib_copy(it, d, hop, j).wait_send()

        def far(h):
            @pl.when(h != g)
            def _():
                far_copy(it, h).wait_send()

        loop(ng, far)

    def tb_copy(i):
        return remote(mytb, tb.at[c, z], tb_s.at[i], tb_r.at[z], (g, i * 2 + c))

    def tb_here(i):
        return remote(mytb, tb.at[c, i], tb_s.at[i], tb_r.at[i], (g, i * 2 + c))

    def tbx(core):
        return remote(tb.at[core], tb.at[core], tbx_s.at[0], tbx_r.at[0], sib)

    def others(n, me, body):
        def step(i):
            @pl.when(i != me)
            def _():
                body(i)

        loop(n, step)

    owner = (g < pieces) & (c == lax.rem(g, 2))
    mine = pl.ds(pl.multiple_of(lax.rem(g, pieces) * prow, 8), prow)

    def piece(j):
        return pl.ds(pl.multiple_of(j * prow, 8), prow)

    def rs_copy(k, j):
        return remote(pay.at[k, piece(j)], rsb.at[k, m], rs_s.at[k, j], rs_r.at[k, m], (j, z * 2 + lax.rem(j, 2)))

    def rs_here(k, i):
        return remote(pay.at[k, mine], rsb.at[k, i], rs_s.at[k, 0], rs_r.at[k, i], sib)

    def z_copy(k, i):
        return remote(zb.at[k, z], zb.at[k, z], z_s.at[k, i], z_r.at[k, z], (g, i * 2 + c))

    def z_here(k, i):
        return remote(zb.at[k, i], zb.at[k, i], z_s.at[k, i], z_r.at[k, i], sib)

    def ag_copy(k, i):
        return remote(res.at[k, mine], res.at[k, mine], ag_s.at[k, i], ag_r.at[k, lax.rem(g, pieces)], plane_dev(i))

    def ag_here(k, j):
        return remote(res.at[k, piece(j)], res.at[k, piece(j)], ag_s.at[k, j], ag_r.at[k, j], sib)

    def is_mine(j):
        return (g == j) & (c == lax.rem(j, 2))

    def sum_start(k):
        def step(j):
            @pl.when(is_mine(j))
            def _():
                rsb[k, m] = pay[k, piece(j)]

            @pl.when(jnp.logical_not(is_mine(j)))
            def _():
                rs_copy(k, j).start()

        loop(pieces, step)

    def sum_plane(k):
        @pl.when(owner)
        def _():
            others(2 * ng, m, lambda i: rs_here(k, i).wait_recv())
            zb[k, z] = functools.reduce(jnp.add, [rsb[k, i] for i in range(2 * ng)])
            others(nz, z, lambda i: z_copy(k, i).start())

    def sum_z(k):
        @pl.when(owner)
        def _():
            others(nz, z, lambda i: z_here(k, i).wait_recv())
            res[k, mine] = functools.reduce(jnp.add, [zb[k, i] for i in range(nz)])
            others(2 * ng, m, lambda i: ag_copy(k, i).start())

    def sum_end(k):
        def step(j):
            @pl.when(jnp.logical_not(is_mine(j)))
            def _():
                ag_here(k, j).wait_recv()

        loop(pieces, step)

    def sum_drain(k):
        def step(j):
            @pl.when(jnp.logical_not(is_mine(j)))
            def _():
                rs_copy(k, j).wait_send()

        loop(pieces, step)

        @pl.when(owner)
        def _():
            others(nz, z, lambda i: z_copy(k, i).wait_send())
            others(2 * ng, m, lambda i: ag_copy(k, i).wait_send())

    def put_sums(k, wide, square):
        pay[k, 0:K, :] = wide
        pay[k, K : K + K // 2, 0:K] = square[0 : K // 2]
        pay[k, K : K + K // 2, K : 2 * K] = square[K // 2 : K]

    def get_sums(k):
        scale = 1.0 / total_rows
        left = res[k, 0:K, 0:K] * scale
        right = res[k, 0:K, K : 2 * K] * scale
        square = jnp.concatenate(
            [res[k, K : K + K // 2, 0:K], res[k, K : K + K // 2, K : 2 * K]], axis=0
        )
        return left, right, square * scale

    def order_tiles():
        iv[...] = jnp.zeros((8, 128), I32)
        iv[0:2, 0:slots] = meta[...]
        lane = lax.broadcasted_iota(I32, (128, 128), 1)
        subl = lax.broadcasted_iota(I32, (128, 128), 0)
        row_r = jnp.broadcast_to(iv[0:1, :], (128, 128))
        slot_r = jnp.broadcast_to(iv[1:2, :], (128, 128))
        key_r = jnp.where(lane < count[0], row_r * 128 + lane, 2048 + lane)
        row_c, slot_c, key_c = row_r.T, slot_r.T, key_r.T
        rank_r = jnp.sum(jnp.where(key_c < key_r, 1, 0), axis=0, keepdims=True)
        hit = jnp.broadcast_to(rank_r, (128, 128)).T == lane
        tile_at = jnp.sum(jnp.where(hit, subl, 0), axis=0, keepdims=True)
        slot_at = jnp.sum(jnp.where(hit, slot_c, 0), axis=0, keepdims=True)
        row_at = jnp.sum(jnp.where(hit, row_c, 0), axis=0, keepdims=True)
        upto = jnp.where((key_c < 2048) & (row_c <= lane), 1, 0)
        end_at = jnp.sum(upto, axis=0, keepdims=True)
        ov[...] = jnp.zeros((8, 128), I32)
        for i, x in enumerate((tile_at, slot_at, row_at, end_at)):
            ov[i : i + 1, :] = x
        cp = pltpu.make_async_copy(ov, sm_iv, loc_sem.at[1])
        cp.start()
        cp.wait()

    def read_tables():
        tbx(1 - c).wait_recv()
        for i in range(2 * nz):
            tv[i : i + 1, :] = tb[i % 2, i // 2, 0:1, :]
        cp = pltpu.make_async_copy(tv, sm_tv, loc_sem.at[2])
        cp.start()
        cp.wait()

        def step(i):
            e = jnp.clip(sm_iv[1, i], 0, RB + 4 * nz + 2 * ng - 1)
            p = jnp.clip((e - RB) // 2, 0, 2 * nz - 1)
            q = jnp.clip(sm_tv[p, 2 * r + e % 2], 0, RB - 1)
            near = p * RB + q
            far = far0 + jnp.clip(e - RB - 4 * nz, 0, 2 * ng - 1)
            sm_ix[i] = jnp.where(e < RB, r * RB + e, jnp.where(e < RB + 4 * nz, near, far))

        loop(slots, step)

    def tile_products(it):
        def step(k, carry):
            acc, prev = carry
            for u in range(UNROLL):
                i = k * UNROLL + u
                row = sm_iv[2, i]
                keep = jnp.where(row == prev, 1.0, 0.0).astype(F32)
                acc = acc * keep + dot16(blk[it, sm_ix[i]], tl[jnp.clip(sm_iv[0, i], 0, slots - 1)], 1, 1)
                runs[i] = acc
                prev = row
            return acc, prev

        lax.fori_loop(0, slots // UNROLL, step, (jnp.zeros((K, BS), F32), jnp.int32(-1)))
        for b in range(RB):
            end = sm_iv[3, b]
            before = sm_iv[3, b - 1] if b else jnp.int32(0)
            some = jnp.where(end > before, 1.0, 0.0).astype(F32)
            hi, lo = split(runs[jnp.clip(end - 1, 0, slots - 1)] * some)
            sh[2 * K : 3 * K, b * BS : (b + 1) * BS] = hi
            sl[2 * K : 3 * K, b * BS : (b + 1) * BS] = lo

    for it in range(ITERS):
        k0, k1 = 2 * it, 2 * it + 1
        if it:
            put_vectors(it)
        start_exchange(it)
        if it == 0:
            others(nz, z, lambda i: tb_copy(i).start())
        put_sums(
            k0,
            dot3(sh[0:K], sl[0:K], sh[0 : 2 * K], sl[0 : 2 * K], 1, 1),
            dot3(sh[K : 2 * K], sl[K : 2 * K], sh[K : 2 * K], sl[K : 2 * K], 1, 1),
        )
        sum_start(k0)
        state = {}
        for hop in range(1, hops + 1):
            ring_step(it, hop)
            if hop == 1:
                sum_plane(k0)
                if it == 0:
                    order_tiles()
            if hop == 2:
                sum_z(k0)
                if it == 0:
                    others(nz, z, lambda i: tb_here(i).wait_recv())
                    tbx(c).start()
        sum_end(k0)
        if it == 0:
            read_tables()
            tile_load.wait()
        g_vv, g_vd, g_dd = get_sums(k0)
        elim = Eliminate(g_vv, work)
        for p in range(K // 8):
            elim.panel(p)
        e_v = elim.inverse()
        u_d = dot32(e_v, g_vd, 1, 0)
        s_dd = g_dd - dot32(u_d, u_d, 0, 0)

        finish_exchange(it)
        tile_products(it)
        put_sums(
            k1,
            dot3(sh[2 * K : 3 * K], sl[2 * K : 3 * K], sh[0 : 2 * K], sl[0 : 2 * K], 1, 1),
            dot3(sh[2 * K : 3 * K], sl[2 * K : 3 * K], sh[2 * K : 3 * K], sl[2 * K : 3 * K], 1, 1),
        )
        sum_start(k1)
        sum_plane(k1)
        sum_z(k1)
        sum_end(k1)
        g_av, g_ad, g_aa = get_sums(k1)
        u_a = dot32(e_v, g_av, 1, 1)
        s_aa = g_aa - dot32(u_a, u_a, 0, 0)
        s_ad = g_ad - dot32(u_a, u_d, 0, 0)
        elim = Eliminate(s_aa, work)
        for p in range(K // 8):
            elim.panel(p)
        e_a = elim.inverse()
        u_ad = dot32(e_a, s_ad, 1, 0)
        elim = Eliminate(s_dd - dot32(u_ad, u_ad, 0, 0), work)
        for p in range(K // 8):
            elim.panel(p)
        e_d = elim.inverse()
        a_v = -dot32(e_a, dot32(u_a, e_v, 0, 0), 1, 0)
        d_v = -dot32(e_d, dot32(u_d, e_v, 0, 0) + dot32(u_ad, a_v, 0, 0), 1, 0)
        d_a = -dot32(e_d, dot32(u_ad, e_a, 0, 0), 1, 0)
        rz_v, rz_a, rz_d = (ritz[it, i * K : (i + 1) * K, :] for i in range(3))
        c_v = dot32(rz_v, e_v, 0, 0) + dot32(rz_a, a_v, 0, 0) + dot32(rz_d, d_v, 0, 0)
        c_a = dot32(rz_a, e_a, 0, 0) + dot32(rz_d, d_a, 0, 0)
        c_d = dot32(rz_d, e_d, 0, 0)
        ch, cl = split(jnp.concatenate([c_v, c_d, c_a], axis=1))
        new = dot3(ch, cl, sh[...], sl[...], 1, 0)
        if it + 1 < ITERS:
            split_into(0, new[0:K])
            split_into(K, new[K : 2 * K])
        else:
            out_v[...] = new[0:K]
            out_d[...] = new[K : 2 * K]

    others(nz, z, lambda i: tb_copy(i).wait_send())
    tbx(c).wait_send()
    for it in range(ITERS):
        drain_exchange(it)
    for k in range(2 * ITERS):
        sum_drain(k)


def shards(ng, nr, sv, sd, tiles, tile_row, tile_slot, tile_count, send_row, send_grp, ritz):
    nz = nr // 2
    slots = tiles.shape[0]
    width = sv.shape[1]
    nblk = 2 * nz * RB + 2 * ng
    hops = nz // 2
    pieces = 12 if ng >= 12 else 3
    prow = 96 // pieces
    calls = 2 * ITERS
    dma = pltpu.SemaphoreType.DMA
    vmem, smem = pl.BlockSpec(memory_space=pltpu.VMEM), pl.BlockSpec(memory_space=pltpu.SMEM)
    return pl.pallas_call(
        functools.partial(kernel, ng, nz, width * ng * nr, slots),
        out_shape=[jax.ShapeDtypeStruct(sv.shape, F32)] * 2,
        in_specs=[vmem, vmem, pl.BlockSpec(memory_space=pl.ANY), vmem, smem, vmem, smem, vmem],
        out_specs=[vmem, vmem],
        scratch_shapes=[
            pltpu.VMEM((ITERS, nblk, K, BS), BF16),
            pltpu.VMEM((ITERS, 2 * ng, K, BS), BF16),
            pltpu.VMEM((RB, K, BS), BF16),
            pltpu.VMEM(tiles.shape, BF16),
            pltpu.VMEM((slots, K, BS), F32),
            pltpu.VMEM((3 * K, width), BF16),
            pltpu.VMEM((3 * K, width), BF16),
            pltpu.VMEM((8, 128), I32),
            pltpu.VMEM((8, 128), I32),
            pltpu.SMEM((8, 128), I32),
            pltpu.SMEM((128,), I32),
            pltpu.VMEM((8, 128), I32),
            pltpu.VMEM((2, nz, 8, 128), I32),
            pltpu.VMEM((2 * nz, 128), I32),
            pltpu.SMEM((2 * nz, 128), I32),
            pltpu.VMEM((calls, 96, 128), F32),
            pltpu.VMEM((calls, 2 * ng, prow, 128), F32),
            pltpu.VMEM((calls, nz, prow, 128), F32),
            pltpu.VMEM((calls, 96, 128), F32),
            pltpu.VMEM((K, 2 * K), F32),
            dma((3,)),
            dma((ITERS, 2, hops, NCH)),
            dma((ITERS, 2, hops, NCH)),
            dma((ITERS, 2, hops + 1, NCH)),
            dma((ITERS, 2, hops + 1, NCH)),
            dma((ITERS, ng)),
            dma((ITERS, ng)),
            dma((nz,)),
            dma((nz,)),
            dma((1,)),
            dma((1,)),
            dma((calls, pieces)),
            dma((calls, 2 * ng)),
            dma((calls, nz)),
            dma((calls, nz)),
            dma((calls, 2 * ng)),
            dma((calls, pieces)),
        ],
        compiler_params=pltpu.CompilerParams(
            collective_id=0, has_side_effects=True, vmem_limit_bytes=48 * 1024 * 1024
        ),
    )(
        sv, sd, tiles, jnp.stack([tile_row, tile_slot]), tile_count,
        send_row.reshape(1, -1), send_grp, ritz,
    )


def solution(mesh):
    spread = P(None, ("grp", "row"))
    flat = P(("grp", "row"))
    return jax.shard_map(
        functools.partial(shards, mesh.shape["grp"], mesh.shape["row"]),
        mesh=mesh,
        in_specs=(spread, spread, P(("grp", "row"), None, None)) + (flat,) * 5 + (P(),),
        out_specs=(spread, spread),
        check_vma=False,
    )
```

```python
import functools

import jax
import jax.numpy as jnp
from jax import lax
from jax.experimental import pallas as pl
from jax.experimental.pallas import tpu as pltpu
from jax.sharding import PartitionSpec as P

ITERS = 2
K = 64
BS = 128
RB = 8
NCH = 4
BPC = RB // NCH
F32, BF16, I32 = jnp.float32, jnp.bfloat16, jnp.int32
MESH = pl.DeviceIdType.MESH
HIGH = lax.Precision.HIGHEST


def dot32(a, b, ca, cb):
    return lax.dot_general(
        a, b, (((ca,), (cb,)), ((), ())), precision=HIGH, preferred_element_type=F32
    )


def dot16(a, b, ca, cb):
    return lax.dot_general(a, b, (((ca,), (cb,)), ((), ())), preferred_element_type=F32)


def split(x):
    hi = x.astype(BF16)
    return hi, (x - hi.astype(F32)).astype(BF16)


def dot3(ah, al, bh, bl, ca, cb):
    return dot16(ah, bh, ca, cb) + (dot16(ah, bl, ca, cb) + dot16(al, bh, ca, cb))


class Eliminate:
    def __init__(self, s, work):
        row = lax.broadcasted_iota(I32, (K, K), 0)
        col = lax.broadcasted_iota(I32, (K, K), 1)
        work[:, 0:K] = s
        work[:, K : 2 * K] = jnp.where(row == col, 1.0, 0.0).astype(F32)
        self.rows = [work[8 * i : 8 * i + 8, :] for i in range(K // 8)]
        self.sub = lax.broadcasted_iota(I32, (8, 2 * K), 0)

    def panel(self, p):
        rows, sub = self.rows, self.sub
        wide = (8, 2 * K)
        cols = [
            [
                jnp.broadcast_to(rows[i][:, 8 * p + k : 8 * p + k + 1], wide)
                for i in range(p, K // 8)
            ]
            for k in range(8)
        ]
        for k in range(8):
            inv = lax.rsqrt(jnp.broadcast_to(cols[k][0][k : k + 1, :], wide))
            low = [c * inv for c in cols[k]]
            for j in range(k + 1, 8):
                mult = jnp.broadcast_to(low[0][j : j + 1, :], wide)
                cols[j] = [c - x * mult for c, x in zip(cols[j], low)]
            pivot = jnp.broadcast_to(rows[p][k : k + 1, :], wide) * inv
            below = jnp.where(sub > k, low[0], 0.0)
            rows[p] = jnp.where(sub == k, pivot, rows[p] - below * pivot)
            for i in range(p + 1, K // 8):
                rows[i] = rows[i] - low[i - p] * pivot

    def inverse(self):
        return jnp.concatenate([r[:, K : 2 * K] for r in self.rows], axis=0)


def eliminate(s, work):
    elim = Eliminate(s, work)
    for p in range(K // 8):
        elim.panel(p)
    return elim.inverse()


def tree_sum(xs):
    while len(xs) > 1:
        xs = [a + b for a, b in zip(xs[0::2], xs[1::2])] + ([xs[-1]] if len(xs) % 2 else [])
    return xs[0]


def near_positions(nz):
    return 2 * (nz // 2 * 5 // 8) + 1


def kernel(
    ng, nz, total_rows, slots,
    sv, sd, tiles, tile_row, tile_slot, count, send_row, send_grp, ritz,
    out_v, out_d,
    blk_a, blk_b, pack, own, tl, runs_a, runs_b, sh, sl, fd, rz, row_in, slot_in, row_list, iv, ov, sm_iv, sm_ix, sm_far,
    mytb, tb, tv, sm_tv, pay, rsb, zb, res, work,
    loc_sem, ring_s, ring_r, sib_s, sib_r, far_s, far_r, tb_s, tb_r, tbx_s, tbx_r,
    rs_s, rs_r, z_s, z_r, ag_s, ag_r,
):
    hops, pos_a = nz // 2, near_positions(nz)
    far0 = pos_a * 2 * RB
    rows_a, rows_b = far0 + 2 * ng, (nz - pos_a) * 2 * RB
    len_a, len_b = runs_a.shape[0], runs_b.shape[0]
    pieces = 12 if ng >= 12 else 3
    prow = 96 // pieces
    side = round(ng**0.5)
    g, r = lax.axis_index("grp"), lax.axis_index("row")
    z, c = r // 2, r % 2
    gx, gy = g // side, g % side
    m = g * 2 + c
    sib = (g, z * 2 + (1 - c))

    def remote(src, dst, ss, rs, dev):
        return pltpu.make_async_remote_copy(
            src_ref=src, dst_ref=dst, send_sem=ss, recv_sem=rs, device_id=dev, device_id_type=MESH
        )

    def wrap(i, n):
        return jnp.where(i >= n, i - n, i)

    z_steps = sorted(range(1, nz), key=lambda k: -min(k, nz - k))
    plane_steps = sorted(
        [(i, j, k) for i in range(side) for j in range(side) for k in range(2) if (i, j, k) != (0, 0, 0)],
        key=lambda t: -min(t[0], side - t[0]) - min(t[1], side - t[1]),
    )

    def z_dev(k):
        return (g, wrap(z + k, nz) * 2 + c)

    def plane_dev(t):
        core = 1 - c if t[2] else c
        return (wrap(gx + t[0], side) * side + wrap(gy + t[1], side), z * 2 + core)

    loads = [
        pltpu.make_async_copy(src, dst, loc_sem.at[i])
        for i, (src, dst) in enumerate(
            [(sv, out_v), (sd, fd), (tiles, tl), (tile_row, row_in), (tile_slot, slot_in),
             (send_row, row_list), (send_grp, sm_far), (ritz, rz)]
        )
    ]
    for cp in loads:
        cp.start()

    barrier = pltpu.get_barrier_semaphore()
    for k in z_steps:
        pl.semaphore_signal(barrier, inc=1, device_id=z_dev(k), device_id_type=MESH)
    for t in plane_steps:
        pl.semaphore_signal(barrier, inc=1, device_id=plane_dev(t), device_id_type=MESH)

    def place(d, hop):
        if hop == 0:
            return 0
        return nz - 1 if hop == hops else 2 * hop - 1 + d

    def chunk(it, pos, core, j=0, n=RB):
        if pos < pos_a:
            return blk_a.at[it, pl.ds(pos * 2 * RB + core * RB + j * BPC, n)]
        return blk_b.at[it, pl.ds((pos - pos_a) * 2 * RB + core * RB + j * BPC, n)]

    def ring_copy(it, d, hop, j):
        to = z_dev(1) if d == 0 else z_dev(nz - 1)
        return remote(
            chunk(it, place(d, hop - 1), c, j, BPC), chunk(it, place(d, hop), c, j, BPC),
            ring_s.at[it, d], ring_r.at[it, d, hop - 1, j], to,
        )

    def ring_here(it, d, hop, j):
        ref = chunk(it, place(d, hop), c, j, BPC)
        return remote(ref, ref, ring_s.at[it, d], ring_r.at[it, d, hop - 1, j], sib)

    def sib_copy(it, d, hop):
        pos = place(d, hop)
        half = hop == hops
        ref = chunk(it, pos, c, NCH // 2 if half and d else 0, RB // 2 if half else RB)
        return remote(ref, ref, sib_s.at[it], sib_r.at[it, int(pos >= pos_a)], sib)

    def ring_has(d, hop, j):
        return hop < hops or (hop == hops and (j < NCH // 2) == (d == 0))

    def far_copy(it, t):
        dev = plane_dev(t)
        return remote(
            pack.at[it, pl.ds(dev[0] * 2, 2)], blk_a.at[it, pl.ds(far0 + 2 * g, 2)],
            far_s.at[it], far_r.at[it], dev,
        )

    far_steps = [t for t in plane_steps if t[2] == 0]

    def drain_exchange(it):
        a, n = blk_a.at[it, pl.ds(0, nz * RB)], (hops - 1) * RB + RB // 2
        remote(a, a, sib_s.at[it], sib_r.at[it, 0], sib).wait_send()
        part = blk_a.at[it, pl.ds(0, n)]
        for d in range(2):
            remote(part, part, ring_s.at[it, d], ring_r.at[it, d, 0, 0], sib).wait_send()
        part = pack.at[it, pl.ds(0, 2 * ng - 2)]
        remote(part, part, far_s.at[it], far_r.at[it], sib).wait_send()

    owner = (g < pieces) & (c == lax.rem(g, 2))
    mine = pl.ds(pl.multiple_of(lax.rem(g, pieces) * prow, 8), prow)

    def is_mine(j):
        return (g == j) & (c == j % 2)

    def either(yes, no):
        @pl.when(owner)
        def _():
            yes()

        @pl.when(jnp.logical_not(owner))
        def _():
            no()

    def sum_start(k):
        for j in range(pieces):
            ref = pay.at[k, j * prow : (j + 1) * prow]

            @pl.when(is_mine(j))
            def _():
                rsb[k, m] = ref[...]

            @pl.when(jnp.logical_not(is_mine(j)))
            def _():
                remote(ref, rsb.at[k, m], rs_s.at[k], rs_r.at[k], (j, z * 2 + j % 2)).start()

    def sum_plane(k):
        @pl.when(owner)
        def _():
            ref = rsb.at[k, 0 : 2 * ng - 1]
            remote(ref, ref, rs_s.at[k], rs_r.at[k], sib).wait_recv()
            zb[k, z] = tree_sum([rsb[k, i] for i in range(2 * ng)])
            for s in z_steps:
                remote(zb.at[k, z], zb.at[k, z], z_s.at[k], z_r.at[k], z_dev(s)).start()

    def sum_z(k):
        @pl.when(owner)
        def _():
            ref = zb.at[k, 0 : nz - 1]
            remote(ref, ref, z_s.at[k], z_r.at[k], sib).wait_recv()
            res[k, mine] = tree_sum([zb[k, i] for i in range(nz)])
            for t in plane_steps:
                remote(res.at[k, mine], res.at[k, mine], ag_s.at[k], ag_r.at[k], plane_dev(t)).start()

    def sum_end(k):
        def wait(n):
            ref = res.at[k, 0 : n * prow]
            remote(ref, ref, ag_s.at[k], ag_r.at[k], sib).wait_recv()

        either(lambda: wait(pieces - 1), lambda: wait(pieces))

    def sum_drain(k):
        def wait(ref, sem):
            remote(ref, ref, sem, ag_r.at[k], sib).wait_send()

        def yes():
            wait(pay.at[k, 0 : (pieces - 1) * prow], rs_s.at[k])
            wait(zb.at[k, 0 : nz - 1], z_s.at[k])
            wait(rsb.at[k, 0 : 2 * ng - 1], ag_s.at[k])

        either(yes, lambda: wait(pay.at[k], rs_s.at[k]))

    def put_sums(k, wide, square):
        pay[k, 0:K, :] = wide
        pay[k, K : K + K // 2, 0:K] = square[0 : K // 2]
        pay[k, K : K + K // 2, K : 2 * K] = square[K // 2 : K]

    def get_sums(k):
        scale = 1.0 / total_rows
        left = res[k, 0:K, 0:K] * scale
        right = res[k, 0:K, K : 2 * K] * scale
        square = jnp.concatenate(
            [res[k, K : K + K // 2, 0:K], res[k, K : K + K // 2, K : 2 * K]], axis=0
        )
        return left, right, square * scale

    def order_tiles():
        loads[3].wait()
        loads[4].wait()
        iv[...] = jnp.zeros((8, 128), I32)
        iv[0:1, 0:slots] = row_in[...]
        iv[1:2, 0:slots] = slot_in[...]
        lane = lax.broadcasted_iota(I32, (128, 128), 1)
        subl = lax.broadcasted_iota(I32, (128, 128), 0)
        row_r = jnp.broadcast_to(iv[0:1, :], (128, 128))
        slot_r = jnp.broadcast_to(iv[1:2, :], (128, 128))
        step = lax.shift_right_arithmetic(slot_r - RB, 2) - z
        step = jnp.where(step < 0, step + nz, step)
        late = (slot_r >= RB) & (slot_r < RB + 4 * nz)
        late = late & (jnp.minimum(step, nz - step) * 2 >= pos_a)
        key_r = jnp.where(late, 1024, 0) + row_r * 128 + lane
        key_r = jnp.where(lane < count[0], key_r, 4096 + lane)
        row_c, slot_c, key_c = row_r.T, slot_r.T, key_r.T
        rank_r = jnp.sum(jnp.where(key_c < key_r, 1, 0), axis=0, keepdims=True)
        hit = jnp.broadcast_to(rank_r, (128, 128)).T == lane

        def total(x):
            return jnp.sum(x, axis=0, keepdims=True)

        ov[...] = jnp.zeros((8, 128), I32)
        ov[0:1, :] = total(jnp.where(hit, subl, 0))
        ov[1:2, :] = total(jnp.where(hit, slot_c, 0))
        ov[2:3, :] = total(jnp.where(hit, row_c, 0))
        ov[3:4, :] = total(jnp.where((key_c < 1024) & (row_c <= lane), 1, 0))
        ov[4:5, :] = total(jnp.where((key_c >= 1024) & (key_c < 4096) & (row_c <= lane), 1, 0))
        pltpu.make_async_copy(ov, sm_iv, loc_sem.at[8]).start()

    def send_table():
        loads[5].wait()
        mytb[...] = jnp.zeros((8, 128), I32)
        mytb[0:1, 0 : 4 * nz] = row_list[...]
        tb[c, z] = mytb[...]
        for k in z_steps:
            remote(mytb, tb.at[c, z], tb_s.at[0], tb_r.at[0], z_dev(k)).start()

    def pass_table():
        ref = tb.at[0, 0 : nz - 1]
        remote(ref, ref, tb_s.at[0], tb_r.at[0], sib).wait_recv()
        remote(tb.at[c], tb.at[c], tbx_s.at[0], tbx_r.at[0], sib).start()

    def take_table():
        remote(tb.at[1 - c], tb.at[1 - c], tbx_s.at[0], tbx_r.at[0], sib).wait_recv()
        for i in range(2 * nz):
            tv[i : i + 1, :] = tb[i % 2, i // 2, 0:1, :]
        pltpu.make_async_copy(tv, sm_tv, loc_sem.at[9]).start()

    def read_table():
        pltpu.make_async_copy(ov, sm_iv, loc_sem.at[8]).wait()
        pltpu.make_async_copy(tv, sm_tv, loc_sem.at[9]).wait()

    def index_tiles(first, last):
        def step(i, carry):
            e = jnp.clip(sm_iv[1, i], 0, RB + 4 * nz + 2 * ng - 1)
            p = jnp.clip(lax.shift_right_arithmetic(e - RB, 1), 0, 2 * nz - 1)
            q = jnp.clip(sm_tv[p, 2 * r + (e & 1)], 0, RB - 1)
            away = lax.shift_right_arithmetic(p, 1) - z
            away = jnp.where(away < 0, away + nz, away)
            pos = jnp.where(away < hops, 2 * away, 2 * (nz - away) - 1)
            pos = jnp.where(pos >= pos_a, pos - pos_a, pos)
            near = pos * 2 * RB + (p & 1) * RB + q
            far = far0 + jnp.clip(e - RB - 4 * nz, 0, 2 * ng - 1)
            sm_ix[i] = jnp.where(e < RB, c * RB + e, jnp.where(e < RB + 4 * nz, near, far))
            return carry

        lax.fori_loop(first, last, step, 0)

    def tile_step(acc, block, i, fresh):
        product = dot16(block, tl[jnp.clip(sm_iv[0, i], 0, slots - 1)], 1, 1)
        if fresh:
            return product
        keep = jnp.where(sm_iv[2, i] == sm_iv[2, i - 1], 1.0, 0.0).astype(F32)
        return acc * keep + product

    def tiles_early(it, state, first, last):
        acc = state.get("acc")
        for i in range(first, min(last, len_a)):
            acc = tile_step(acc, blk_a[it, jnp.clip(sm_ix[i], 0, rows_a - 1)], i, i == 0)
            runs_a[i] = acc
        state["acc"] = acc

    def tiles_late(it):
        first, acc = jnp.clip(sm_iv[3, RB - 1], 0, len_a), None
        for u in range(len_b):
            i = first + u
            acc = tile_step(acc, blk_b[it, jnp.clip(sm_ix[i], 0, rows_b - 1)], i, u == 0)
            runs_b[u] = acc
        for b in range(RB):
            x = 0.0
            for line, runs, size in ((3, runs_a, len_a), (4, runs_b, len_b)):
                end = sm_iv[line, b]
                before = sm_iv[line, b - 1] if b else jnp.int32(0)
                some = jnp.where(end > before, 1.0, 0.0).astype(F32)
                x = x + runs[jnp.clip(end - 1, 0, size - 1)] * some
            hi, lo = split(x)
            sh[2 * K : 3 * K, b * BS : (b + 1) * BS] = hi
            sl[2 * K : 3 * K, b * BS : (b + 1) * BS] = lo

    def split_into(row0, x):
        hi, lo = split(x)
        sh[row0 : row0 + K, :] = hi
        sl[row0 : row0 + K, :] = lo

    def put_vectors(it, x):
        split_into(0, x)
        for b in range(RB):
            part = sh[0:K, b * BS : (b + 1) * BS]
            own[b] = part
            blk_a[it, c * RB + b] = part

    def send_far(it):
        if it == 0:
            loads[6].wait()
        for h in range(ng):
            for s in range(2):
                pack[it, h * 2 + s] = own[jnp.clip(sm_far[h * 2 + s], 0, RB - 1)]
        zero = jnp.zeros((K, BS), BF16)
        blk_a[it, far0 + 2 * g] = zero
        blk_a[it, far0 + 2 * g + 1] = zero
        for t in far_steps:
            far_copy(it, t).start()

    def wait_early(it):
        ref = blk_a.at[it, pl.ds(0, pos_a * RB)]
        remote(ref, ref, sib_s.at[it], sib_r.at[it, 0], sib).wait_recv()
        ref = blk_a.at[it, pl.ds(0, 2 * ng - 2)]
        remote(ref, ref, far_s.at[it], far_r.at[it], sib).wait_recv()

    def wait_late(it):
        ref = blk_b.at[it, pl.ds(0, (nz - pos_a) * RB)]
        remote(ref, ref, sib_s.at[it], sib_r.at[it, 1], sib).wait_recv()

    def first_products():
        put_sums(
            0,
            dot3(sh[0:K], sl[0:K], sh[0 : 2 * K], sl[0 : 2 * K], 1, 1),
            dot3(sh[K : 2 * K], sl[K : 2 * K], sh[K : 2 * K], sl[K : 2 * K], 1, 1),
        )

    def get_directions(it):
        if it == 0:
            loads[1].wait()
        split_into(K, fd[...])

    loads[0].wait()
    put_vectors(0, out_v[...])
    pl.semaphore_wait(barrier, nz - 1 + 2 * ng - 1)

    for it in range(ITERS):
        k0, k1 = 0, 1 + it
        for j in range(NCH):
            for d in range(2):
                ring_copy(it, d, 1, j).start()
        sib_copy(it, 0, 0).start()

        state = {}
        early = hops * 5 // 8 * NCH + 1
        ready = early - max(1, NCH // 2)
        last = (hops - 1) * NCH + NCH // 2
        plan = [(0, functools.partial(send_far, it)), (1, functools.partial(get_directions, it))]
        if it == 0:
            mid = ready // 2 + 1
            tail = max(mid + 2, ready - 4)
            plan += [
                (0, send_table),
                (2, first_products),
                (2, functools.partial(sum_start, k0)),
                (3, order_tiles),
                (mid, functools.partial(sum_plane, k0)),
                (mid + 1, pass_table),
                (tail, take_table),
                (tail + 1, read_table),
                (max(mid + 2, last - 4), functools.partial(sum_z, k0)),
            ]
            part = -(-slots // 3)
            for i in range(3):
                plan += [(tail + 1 + i, functools.partial(index_tiles, i * part, min(slots, (i + 1) * part)))]
            early = max(early, tail + 4)
        plan += [(early, functools.partial(wait_early, it))]
        if it == 0:
            plan += [(early, lambda: loads[2].wait())]
        part = -(-len_a // max(1, last - early))
        for i in range(-(-len_a // part)):
            plan += [(early + i, functools.partial(tiles_early, it, state, i * part, (i + 1) * part))]
        plan = sorted(enumerate(plan), key=lambda t: (t[1][0], t[0]))
        plan = [t[1] for t in plan]

        step = 0
        for hop in range(1, hops + 1):
            for j in range(NCH):
                for d in range(2):
                    if ring_has(d, hop, j):
                        ring_here(it, d, hop, j).wait_recv()
                        if ring_has(d, hop + 1, j):
                            ring_copy(it, d, hop + 1, j).start()
                        if not ring_has(d, hop, j + 1) or j == NCH - 1:
                            sib_copy(it, d, hop).start()
                while plan and plan[0][0] <= step:
                    plan.pop(0)[1]()
                step += 1
        for _, work_left in plan:
            work_left()
        wait_late(it)
        tiles_late(it)
        put_sums(
            k1,
            dot3(sh[2 * K : 3 * K], sl[2 * K : 3 * K], sh[0 : 2 * K], sl[0 : 2 * K], 1, 1),
            dot3(sh[2 * K : 3 * K], sl[2 * K : 3 * K], sh[2 * K : 3 * K], sl[2 * K : 3 * K], 1, 1),
        )
        sum_start(k1)
        if it == 0:
            sum_end(k0)
            g_vv, g_vd, g_dd = get_sums(k0)
            loads[7].wait()
        else:
            before = rz[it - 1]
            wide = dot32(before, before, 0, 0)
            g_vv, g_vd, g_dd = wide[0:K, 0:K], wide[0:K, K : 2 * K], wide[K : 2 * K, K : 2 * K]
        e_v = eliminate(g_vv, work)
        u_d = dot32(e_v, g_vd, 1, 0)
        s_dd = g_dd - dot32(u_d, u_d, 0, 0)
        sum_plane(k1)
        d_e = dot32(u_d, e_v, 0, 0)
        sum_z(k1)
        sum_end(k1)
        g_av, g_ad, g_aa = get_sums(k1)
        u_a = dot32(e_v, g_av, 1, 1)
        s_aa = g_aa - dot32(u_a, u_a, 0, 0)
        s_ad = g_ad - dot32(u_a, u_d, 0, 0)
        e_a = eliminate(s_aa, work)
        u_ad = dot32(e_a, s_ad, 1, 0)
        e_d = eliminate(s_dd - dot32(u_ad, u_ad, 0, 0), work)
        a_v = -dot32(e_a, dot32(u_a, e_v, 0, 0), 1, 0)
        d_v = -dot32(e_d, d_e + dot32(u_ad, a_v, 0, 0), 1, 0)
        d_a = -dot32(e_d, dot32(u_ad, e_a, 0, 0), 1, 0)
        rz_v, rz_a, rz_d = (rz[it, i * K : (i + 1) * K, :] for i in range(3))
        c_v = dot32(rz_v, e_v, 0, 0) + dot32(rz_a, a_v, 0, 0) + dot32(rz_d, d_v, 0, 0)
        c_a = dot32(rz_a, e_a, 0, 0) + dot32(rz_d, d_a, 0, 0)
        c_d = dot32(rz_d, e_d, 0, 0)
        ch, cl = split(jnp.concatenate([c_v, c_d, c_a], axis=1))
        if it + 1 < ITERS:
            x = dot3(ch[0:K], cl[0:K], sh[...], sl[...], 1, 0)
            y = dot3(ch[K : 2 * K], cl[K : 2 * K], sh[...], sl[...], 1, 0)
            put_vectors(it + 1, x)
            fd[...] = y
        else:
            new = dot3(ch, cl, sh[...], sl[...], 1, 0)
            out_v[...] = new[0:K]
            out_d[...] = new[K : 2 * K]

    ref = tb.at[0, 0 : nz - 1]
    remote(ref, ref, tb_s.at[0], tb_r.at[0], sib).wait_send()
    remote(tb.at[c], tb.at[c], tbx_s.at[0], tbx_r.at[0], sib).wait_send()
    for it in range(ITERS):
        drain_exchange(it)
    for k in range(1 + ITERS):
        sum_drain(k)


def shards(ng, nr, sv, sd, tiles, tile_row, tile_slot, tile_count, send_row, send_grp, ritz):
    nz = nr // 2
    slots, width = tiles.shape[0], sv.shape[1]
    pos_a = near_positions(nz)
    far0 = pos_a * 2 * RB
    len_a = RB + 2 * (ng - 1) + 2 * (2 * pos_a - 1)
    len_b = 4 * (nz - pos_a)
    pieces = 12 if ng >= 12 else 3
    prow = 96 // pieces
    calls = 1 + ITERS
    dma = pltpu.SemaphoreType.DMA
    vmem, smem = pl.BlockSpec(memory_space=pltpu.VMEM), pl.BlockSpec(memory_space=pltpu.SMEM)
    hbm = pl.BlockSpec(memory_space=pl.ANY)
    return pl.pallas_call(
        functools.partial(kernel, ng, nz, width * ng * nr, slots),
        out_shape=[jax.ShapeDtypeStruct(sv.shape, F32)] * 2,
        in_specs=[hbm] * 5 + [smem] + [hbm] * 3,
        out_specs=[vmem, vmem],
        scratch_shapes=[
            pltpu.VMEM((ITERS, far0 + 2 * ng, K, BS), BF16),
            pltpu.VMEM((ITERS, (nz - pos_a) * 2 * RB, K, BS), BF16),
            pltpu.VMEM((ITERS, 2 * ng, K, BS), BF16),
            pltpu.VMEM((RB, K, BS), BF16),
            pltpu.VMEM(tiles.shape, BF16),
            pltpu.VMEM((len_a, K, BS), F32),
            pltpu.VMEM((len_b, K, BS), F32),
            pltpu.VMEM((3 * K, width), BF16),
            pltpu.VMEM((3 * K, width), BF16),
            pltpu.VMEM((K, width), F32),
            pltpu.VMEM(ritz.shape, F32),
            pltpu.VMEM((1, slots), I32),
            pltpu.VMEM((1, slots), I32),
            pltpu.VMEM((1, 4 * nz), I32),
            pltpu.VMEM((8, 128), I32),
            pltpu.VMEM((8, 128), I32),
            pltpu.SMEM((8, 128), I32),
            pltpu.SMEM((128,), I32),
            pltpu.SMEM(send_grp.shape, I32),
            pltpu.VMEM((8, 128), I32),
            pltpu.VMEM((2, nz, 8, 128), I32),
            pltpu.VMEM((2 * nz, 128), I32),
            pltpu.SMEM((2 * nz, 128), I32),
            pltpu.VMEM((calls, 96, 128), F32),
            pltpu.VMEM((calls, 2 * ng, prow, 128), F32),
            pltpu.VMEM((calls, nz, prow, 128), F32),
            pltpu.VMEM((calls, 96, 128), F32),
            pltpu.VMEM((K, 2 * K), F32),
            dma((10,)),
            dma((ITERS, 2)),
            dma((ITERS, 2, nz // 2, NCH)),
            dma((ITERS,)),
            dma((ITERS, 2)),
            dma((ITERS,)),
            dma((ITERS,)),
            dma((1,)),
            dma((1,)),
            dma((1,)),
            dma((1,)),
            dma((calls,)),
            dma((calls,)),
            dma((calls,)),
            dma((calls,)),
            dma((calls,)),
            dma((calls,)),
        ],
        compiler_params=pltpu.CompilerParams(
            collective_id=0, has_side_effects=True, vmem_limit_bytes=60 * 1024 * 1024
        ),
    )(
        sv, sd, tiles, tile_row.reshape(1, -1), tile_slot.reshape(1, -1), tile_count,
        send_row.reshape(1, -1), send_grp, ritz,
    )


def solution(mesh):
    spread = P(None, ("grp", "row"))
    flat = P(("grp", "row"))
    return jax.shard_map(
        functools.partial(shards, mesh.shape["grp"], mesh.shape["row"]),
        mesh=mesh,
        in_specs=(spread, spread, P(("grp", "row"), None, None)) + (flat,) * 5 + (P(),),
        out_specs=(spread, spread),
        check_vma=False,
    )
```

```python
import functools

import jax
import jax.numpy as jnp
from jax import lax
from jax.experimental import pallas as pl
from jax.experimental.pallas import tpu as pltpu
from jax.sharding import PartitionSpec as P

ITERS = 2
K = 64
BS = 128
RB = 8
NCH = 4
BPC = RB // NCH
F32, BF16, I32 = jnp.float32, jnp.bfloat16, jnp.int32
MESH = pl.DeviceIdType.MESH
HIGH = lax.Precision.HIGHEST


def dot32(a, b, ca, cb):
    return lax.dot_general(
        a, b, (((ca,), (cb,)), ((), ())), precision=HIGH, preferred_element_type=F32
    )


def dot16(a, b, ca, cb):
    return lax.dot_general(a, b, (((ca,), (cb,)), ((), ())), preferred_element_type=F32)


def split(x):
    hi = x.astype(BF16)
    return hi, (x - hi.astype(F32)).astype(BF16)


def dot3(ah, al, bh, bl, ca, cb):
    return dot16(ah, bh, ca, cb) + (dot16(ah, bl, ca, cb) + dot16(al, bh, ca, cb))


class Eliminate:
    def __init__(self, s, work):
        row = lax.broadcasted_iota(I32, (K, K), 0)
        col = lax.broadcasted_iota(I32, (K, K), 1)
        work[:, 0:K] = s
        work[:, K : 2 * K] = jnp.where(row == col, 1.0, 0.0).astype(F32)
        self.rows = [work[8 * i : 8 * i + 8, :] for i in range(K // 8)]
        self.sub = lax.broadcasted_iota(I32, (8, 2 * K), 0)

    def panel(self, p):
        rows, sub = self.rows, self.sub
        wide = (8, 2 * K)
        cols = [
            [
                jnp.broadcast_to(rows[i][:, 8 * p + k : 8 * p + k + 1], wide)
                for i in range(p, K // 8)
            ]
            for k in range(8)
        ]
        for k in range(8):
            inv = lax.rsqrt(jnp.broadcast_to(cols[k][0][k : k + 1, :], wide))
            low = [c * inv for c in cols[k]]
            for j in range(k + 1, 8):
                mult = jnp.broadcast_to(low[0][j : j + 1, :], wide)
                cols[j] = [c - x * mult for c, x in zip(cols[j], low)]
            pivot = jnp.broadcast_to(rows[p][k : k + 1, :], wide) * inv
            below = jnp.where(sub > k, low[0], 0.0)
            rows[p] = jnp.where(sub == k, pivot, rows[p] - below * pivot)
            for i in range(p + 1, K // 8):
                rows[i] = rows[i] - low[i - p] * pivot

    def inverse(self):
        return jnp.concatenate([r[:, K : 2 * K] for r in self.rows], axis=0)


def eliminate(s, work):
    elim = Eliminate(s, work)
    for p in range(K // 8):
        elim.panel(p)
    return elim.inverse()


def tree_sum(xs):
    while len(xs) > 1:
        xs = [a + b for a, b in zip(xs[0::2], xs[1::2])] + ([xs[-1]] if len(xs) % 2 else [])
    return xs[0]


def near_positions(nz):
    return 2 * (nz // 2 * 5 // 8) + 1


def kernel(
    ng, nz, total_rows, slots,
    sv, sd, tiles, tile_row, tile_slot, count, send_row, send_grp, ritz,
    out,
    blk_a, blk_b, pack, own, tl, runs_a, runs_b, sh, sl, fd, rz, row_in, slot_in, row_list, iv, ov, sm_iv, sm_count, sm_far,
    mytb, tb, tv, pay, rsb, zb, res, work,
    loc_sem, ring_s, ring_r, sib_s, sib_r, far_s, far_r, tb_s, tb_r, tbx_s, tbx_r,
    rs_s, rs_r, z_s, z_r, ag_s, ag_r,
):
    hops, pos_a = nz // 2, near_positions(nz)
    far0 = pos_a * 2 * RB
    rows_a, rows_b = far0 + 2 * ng, (nz - pos_a) * 2 * RB
    len_a, len_b = runs_a.shape[0], runs_b.shape[0]
    pieces = 12 if ng >= 12 else 3
    prow = 96 // pieces
    side = round(ng**0.5)
    g, r = lax.axis_index("grp"), lax.axis_index("row")
    z, c = r // 2, r % 2
    gx, gy = g // side, g % side
    m = g * 2 + c
    sib = (g, z * 2 + (1 - c))

    def remote(src, dst, ss, rs, dev):
        return pltpu.make_async_remote_copy(
            src_ref=src, dst_ref=dst, send_sem=ss, recv_sem=rs, device_id=dev, device_id_type=MESH
        )

    def wrap(i, n):
        return jnp.where(i >= n, i - n, i)

    z_steps = sorted(range(1, nz), key=lambda k: -min(k, nz - k))
    plane_steps = sorted(
        [(i, j, k) for i in range(side) for j in range(side) for k in range(2) if (i, j, k) != (0, 0, 0)],
        key=lambda t: -min(t[0], side - t[0]) - min(t[1], side - t[1]),
    )

    def z_dev(k):
        return (g, wrap(z + k, nz) * 2 + c)

    def plane_dev(t):
        core = 1 - c if t[2] else c
        return (wrap(gx + t[0], side) * side + wrap(gy + t[1], side), z * 2 + core)

    loads = [
        pltpu.make_async_copy(src, dst, loc_sem.at[i])
        for i, (src, dst) in enumerate(
            [(sv, out.at[0:K]), (sd, fd), (tiles, tl), (tile_row, row_in), (tile_slot, slot_in),
             (send_row, row_list), (send_grp, sm_far), (ritz, rz), (count, sm_count)]
        )
    ]
    for cp in loads:
        cp.start()

    barrier = pltpu.get_barrier_semaphore()
    for k in z_steps:
        pl.semaphore_signal(barrier, inc=1, device_id=z_dev(k), device_id_type=MESH)
    for t in plane_steps:
        pl.semaphore_signal(barrier, inc=1, device_id=plane_dev(t), device_id_type=MESH)

    def place(d, hop):
        if hop == 0:
            return 0
        return nz - 1 if hop == hops else 2 * hop - 1 + d

    def chunk(it, pos, core, j=0, n=RB):
        if pos < pos_a:
            return blk_a.at[it, pl.ds(pos * 2 * RB + core * RB + j * BPC, n)]
        return blk_b.at[it, pl.ds((pos - pos_a) * 2 * RB + core * RB + j * BPC, n)]

    def ring_copy(it, d, hop, j):
        to = z_dev(1) if d == 0 else z_dev(nz - 1)
        return remote(
            chunk(it, place(d, hop - 1), c, j, BPC), chunk(it, place(d, hop), c, j, BPC),
            ring_s.at[it, d], ring_r.at[it, d, hop - 1, j], to,
        )

    def ring_here(it, d, hop, j):
        ref = chunk(it, place(d, hop), c, j, BPC)
        return remote(ref, ref, ring_s.at[it, d], ring_r.at[it, d, hop - 1, j], sib)

    def sib_copy(it, d, hop):
        pos = place(d, hop)
        half = hop == hops
        ref = chunk(it, pos, c, NCH // 2 if half and d else 0, RB // 2 if half else RB)
        return remote(ref, ref, sib_s.at[it], sib_r.at[it, int(pos >= pos_a)], sib)

    def ring_has(d, hop, j):
        return hop < hops or (hop == hops and (j < NCH // 2) == (d == 0))

    def far_copy(it, t):
        dev = plane_dev(t)
        return remote(
            pack.at[it, pl.ds(dev[0] * 2, 2)], blk_a.at[it, pl.ds(far0 + 2 * g, 2)],
            far_s.at[it], far_r.at[it], dev,
        )

    far_steps = [t for t in plane_steps if t[2] == 0]

    def drain_exchange(it):
        a, n = blk_a.at[it, pl.ds(0, nz * RB)], (hops - 1) * RB + RB // 2
        remote(a, a, sib_s.at[it], sib_r.at[it, 0], sib).wait_send()
        part = blk_a.at[it, pl.ds(0, n)]
        for d in range(2):
            remote(part, part, ring_s.at[it, d], ring_r.at[it, d, 0, 0], sib).wait_send()
        part = pack.at[it, pl.ds(0, 2 * ng - 2)]
        remote(part, part, far_s.at[it], far_r.at[it], sib).wait_send()

    mine = pl.ds(pl.multiple_of(lax.rem(g, pieces) * prow, 8), prow)

    def owner_core(k, j):
        return (j + (k == 0)) % 2

    def owner(k):
        return (g < pieces) & (c == lax.rem(g + (k == 0), 2))

    def is_mine(k, j):
        return (g == j) & (c == owner_core(k, j))

    def either(k, yes, no):
        @pl.when(owner(k))
        def _():
            yes()

        @pl.when(jnp.logical_not(owner(k)))
        def _():
            no()

    def sum_start(k):
        for j in range(pieces):
            ref = pay.at[k, j * prow : (j + 1) * prow]

            @pl.when(is_mine(k, j))
            def _():
                rsb[k, m] = ref[...]

            @pl.when(jnp.logical_not(is_mine(k, j)))
            def _():
                remote(ref, rsb.at[k, m], rs_s.at[k], rs_r.at[k], (j, z * 2 + owner_core(k, j))).start()

    def sum_plane(k):
        @pl.when(owner(k))
        def _():
            ref = rsb.at[k, 0 : 2 * ng - 1]
            remote(ref, ref, rs_s.at[k], rs_r.at[k], sib).wait_recv()
            zb[k, z] = tree_sum([rsb[k, i] for i in range(2 * ng)])
            for s in z_steps:
                remote(zb.at[k, z], zb.at[k, z], z_s.at[k], z_r.at[k], z_dev(s)).start()

    def sum_z(k):
        @pl.when(owner(k))
        def _():
            ref = zb.at[k, 0 : nz - 1]
            remote(ref, ref, z_s.at[k], z_r.at[k], sib).wait_recv()
            res[k, mine] = tree_sum([zb[k, i] for i in range(nz)])
            for t in plane_steps:
                remote(res.at[k, mine], res.at[k, mine], ag_s.at[k], ag_r.at[k], plane_dev(t)).start()

    def sum_end(k):
        def wait(n):
            ref = res.at[k, 0 : n * prow]
            remote(ref, ref, ag_s.at[k], ag_r.at[k], sib).wait_recv()

        either(k, lambda: wait(pieces - 1), lambda: wait(pieces))

    def sum_drain(k):
        def wait(ref, sem):
            remote(ref, ref, sem, ag_r.at[k], sib).wait_send()

        def yes():
            wait(pay.at[k, 0 : (pieces - 1) * prow], rs_s.at[k])
            wait(zb.at[k, 0 : nz - 1], z_s.at[k])
            wait(rsb.at[k, 0 : 2 * ng - 1], ag_s.at[k])

        either(k, yes, lambda: wait(pay.at[k], rs_s.at[k]))

    def put_sums(k, wide, square):
        pay[k, 0:K, :] = wide
        pay[k, K : K + K // 2, 0:K] = square[0 : K // 2]
        pay[k, K : K + K // 2, K : 2 * K] = square[K // 2 : K]

    def get_sums(k):
        scale = 1.0 / total_rows
        left = res[k, 0:K, 0:K] * scale
        right = res[k, 0:K, K : 2 * K] * scale
        square = jnp.concatenate(
            [res[k, K : K + K // 2, 0:K], res[k, K : K + K // 2, K : 2 * K]], axis=0
        )
        return left, right, square * scale

    def order_tiles():
        for i in (3, 4, 8):
            loads[i].wait()
        iv[...] = jnp.zeros((8, 128), I32)
        iv[0:1, 0:slots] = row_in[...]
        iv[1:2, 0:slots] = slot_in[...]
        lane = lax.broadcasted_iota(I32, (128, 128), 1)
        subl = lax.broadcasted_iota(I32, (128, 128), 0)
        row_r = jnp.broadcast_to(iv[0:1, :], (128, 128))
        slot_r = jnp.broadcast_to(iv[1:2, :], (128, 128))
        step = lax.shift_right_arithmetic(slot_r - RB, 2) - z
        step = jnp.where(step < 0, step + nz, step)
        late = (slot_r >= RB) & (slot_r < RB + 4 * nz)
        late = late & (jnp.minimum(step, nz - step) * 2 >= pos_a)
        key_r = jnp.where(late, 1024, 0) + row_r * 128 + lane
        key_r = jnp.where(lane < sm_count[0], key_r, 4096 + lane)
        row_c, slot_c, key_c = row_r.T, slot_r.T, key_r.T
        rank_r = jnp.sum(jnp.where(key_c < key_r, 1, 0), axis=0, keepdims=True)
        hit = jnp.broadcast_to(rank_r, (128, 128)).T == lane

        def total(x):
            return jnp.sum(x, axis=0, keepdims=True)

        ov[...] = jnp.zeros((8, 128), I32)
        ov[0:1, :] = total(jnp.where(hit, subl, 0))
        ov[1:2, :] = total(jnp.where(hit, slot_c, 0))
        ov[2:3, :] = total(jnp.where(hit, row_c, 0))
        ov[3:4, :] = total(jnp.where((key_c < 1024) & (row_c <= lane), 1, 0))
        ov[4:5, :] = total(jnp.where((key_c >= 1024) & (key_c < 4096) & (row_c <= lane), 1, 0))

    def send_table():
        loads[5].wait()
        mytb[...] = jnp.zeros((8, 128), I32)
        mytb[0:1, 0 : 4 * nz] = row_list[...]
        tb[c, z] = mytb[...]
        for k in z_steps:
            remote(mytb, tb.at[c, z], tb_s.at[0], tb_r.at[0], z_dev(k)).start()

    def pass_table():
        ref = tb.at[0, 0 : nz - 1]
        remote(ref, ref, tb_s.at[0], tb_r.at[0], sib).wait_recv()
        remote(tb.at[c], tb.at[c], tbx_s.at[0], tbx_r.at[0], sib).start()

    def take_table():
        remote(tb.at[1 - c], tb.at[1 - c], tbx_s.at[0], tbx_r.at[0], sib).wait_recv()
        tv[...] = jnp.zeros((128, 128), I32)
        for i in range(2 * nz):
            tv[i : i + 1, :] = tb[i % 2, i // 2, 0:1, :]
        tv[...] = tv[...].T

    def index_tiles():
        def column(s):
            return jnp.broadcast_to(tv[pl.ds(2 * r + s, 1), :], (128, 128)).T

        sender = lax.broadcasted_iota(I32, (128, 128), 0)
        e = ov[1:2, :]
        p = lax.shift_right_arithmetic(e - RB, 1)
        listed = jnp.where(jnp.broadcast_to(e & 1, (128, 128)) == 0, column(0), column(1))
        q = jnp.sum(jnp.where(sender == jnp.broadcast_to(p, (128, 128)), listed, 0), axis=0, keepdims=True)
        away = lax.shift_right_arithmetic(p, 1) - z
        away = jnp.where(away < 0, away + nz, away)
        pos = jnp.where(away < hops, 2 * away, 2 * (nz - away) - 1)
        pos = jnp.where(pos >= pos_a, pos - pos_a, pos)
        near = pos * 2 * RB + (p & 1) * RB + q
        far = far0 + e - RB - 4 * nz
        ov[5:6, :] = jnp.where(e < RB, c * RB + e, jnp.where(e < RB + 4 * nz, near, far))
        pltpu.make_async_copy(ov, sm_iv, loc_sem.at[9]).start()

    def read_table():
        pltpu.make_async_copy(ov, sm_iv, loc_sem.at[9]).wait()

    def tile_step(acc, block, i, fresh):
        product = dot16(block, tl[jnp.clip(sm_iv[0, i], 0, slots - 1)], 1, 1)
        if fresh:
            return product
        keep = jnp.where(sm_iv[2, i] == sm_iv[2, i - 1], 1.0, 0.0).astype(F32)
        return acc * keep + product

    def tiles_early(it, state, first, last):
        acc = state.get("acc")
        for i in range(first, min(last, len_a)):
            acc = tile_step(acc, blk_a[it, jnp.clip(sm_iv[5, i], 0, rows_a - 1)], i, i == 0)
            runs_a[i] = acc
        state["acc"] = acc

    def tiles_late(it):
        first, acc = jnp.clip(sm_iv[3, RB - 1], 0, len_a), None
        for u in range(len_b):
            i = first + u
            acc = tile_step(acc, blk_b[it, jnp.clip(sm_iv[5, i], 0, rows_b - 1)], i, u == 0)
            runs_b[u] = acc
        for b in range(RB):
            x = 0.0
            for line, runs, size in ((3, runs_a, len_a), (4, runs_b, len_b)):
                end = sm_iv[line, b]
                before = sm_iv[line, b - 1] if b else jnp.int32(0)
                some = jnp.where(end > before, 1.0, 0.0).astype(F32)
                x = x + runs[jnp.clip(end - 1, 0, size - 1)] * some
            hi, lo = split(x)
            sh[2 * K : 3 * K, b * BS : (b + 1) * BS] = hi
            sl[2 * K : 3 * K, b * BS : (b + 1) * BS] = lo

    def split_into(row0, x):
        hi, lo = split(x)
        sh[row0 : row0 + K, :] = hi
        sl[row0 : row0 + K, :] = lo

    def put_vectors(it, x):
        split_into(0, x)
        for b in range(RB):
            part = sh[0:K, b * BS : (b + 1) * BS]
            own[b] = part
            blk_a[it, c * RB + b] = part

    def send_far(it):
        if it == 0:
            loads[6].wait()
        for h in range(ng):
            for s in range(2):
                pack[it, h * 2 + s] = own[jnp.clip(sm_far[h * 2 + s], 0, RB - 1)]
        zero = jnp.zeros((K, BS), BF16)
        blk_a[it, far0 + 2 * g] = zero
        blk_a[it, far0 + 2 * g + 1] = zero
        for t in far_steps:
            far_copy(it, t).start()

    def wait_early(it):
        ref = blk_a.at[it, pl.ds(0, pos_a * RB)]
        remote(ref, ref, sib_s.at[it], sib_r.at[it, 0], sib).wait_recv()
        ref = blk_a.at[it, pl.ds(0, 2 * ng - 2)]
        remote(ref, ref, far_s.at[it], far_r.at[it], sib).wait_recv()

    def wait_late(it):
        ref = blk_b.at[it, pl.ds(0, (nz - pos_a) * RB)]
        remote(ref, ref, sib_s.at[it], sib_r.at[it, 1], sib).wait_recv()

    def first_products():
        put_sums(
            0,
            dot3(sh[0:K], sl[0:K], sh[0 : 2 * K], sl[0 : 2 * K], 1, 1),
            dot3(sh[K : 2 * K], sl[K : 2 * K], sh[K : 2 * K], sl[K : 2 * K], 1, 1),
        )

    def get_directions(it):
        if it == 0:
            loads[1].wait()
        split_into(K, fd[...])

    loads[0].wait()
    put_vectors(0, out[0:K])
    pl.semaphore_wait(barrier, nz - 1 + 2 * ng - 1)

    for it in range(ITERS):
        k0, k1 = 0, 1 + it
        for j in range(NCH):
            for d in range(2):
                ring_copy(it, d, 1, j).start()
        sib_copy(it, 0, 0).start()

        state = {}
        early = hops * 5 // 8 * NCH + 1
        ready = early - max(1, NCH // 2)
        last = (hops - 1) * NCH + NCH // 2
        plan = [(0, functools.partial(send_far, it)), (1, functools.partial(get_directions, it))]
        if it == 0:
            mid = ready // 2 + 1
            tail = max(mid + 2, ready - 4)
            plan += [
                (0, send_table),
                (2, first_products),
                (2, functools.partial(sum_start, k0)),
                (3, order_tiles),
                (mid, functools.partial(sum_plane, k0)),
                (mid + 1, pass_table),
                (tail, take_table),
                (tail + 1, index_tiles),
                (tail + 3, read_table),
            ]
            early = max(early, tail + 4)
        plan += [(early, functools.partial(wait_early, it))]
        if it == 0:
            plan += [(early, lambda: loads[2].wait())]
        part = -(-len_a // max(1, last - early))
        for i in range(-(-len_a // part)):
            plan += [(early + i, functools.partial(tiles_early, it, state, i * part, (i + 1) * part))]
        plan = sorted(enumerate(plan), key=lambda t: (t[1][0], t[0]))
        plan = [t[1] for t in plan]

        step = 0
        for hop in range(1, hops + 1):
            for j in range(NCH):
                for d in range(2):
                    if ring_has(d, hop, j):
                        ring_here(it, d, hop, j).wait_recv()
                        if ring_has(d, hop + 1, j):
                            ring_copy(it, d, hop + 1, j).start()
                        if not ring_has(d, hop, j + 1) or j == NCH - 1:
                            sib_copy(it, d, hop).start()
                while plan and plan[0][0] <= step:
                    plan.pop(0)[1]()
                step += 1
        for _, work_left in plan:
            work_left()
        wait_late(it)
        tiles_late(it)
        put_sums(
            k1,
            dot3(sh[2 * K : 3 * K], sl[2 * K : 3 * K], sh[0 : 2 * K], sl[0 : 2 * K], 1, 1),
            dot3(sh[2 * K : 3 * K], sl[2 * K : 3 * K], sh[2 * K : 3 * K], sl[2 * K : 3 * K], 1, 1),
        )
        sum_start(k1)
        if it == 0:
            loads[7].wait()
            sum_z(k0)
            sum_plane(k1)
            sum_end(k0)
            g_vv, g_vd, g_dd = get_sums(k0)
        else:
            before = rz[it - 1]
            wide = dot32(before, before, 0, 0)
            g_vv, g_vd, g_dd = wide[0:K, 0:K], wide[0:K, K : 2 * K], wide[K : 2 * K, K : 2 * K]
        rz_v, rz_a, rz_d = (rz[it, i * K : (i + 1) * K, :] for i in range(3))
        e_v = eliminate(g_vv, work)
        u_d = dot32(e_v, g_vd, 1, 0)
        s_dd = g_dd - dot32(u_d, u_d, 0, 0)
        if it:
            sum_plane(k1)
        d_e = dot32(u_d, e_v, 0, 0)
        v_e = dot32(rz_v, e_v, 0, 0)
        sum_z(k1)
        sum_end(k1)
        g_av, g_ad, g_aa = get_sums(k1)
        u_a = dot32(e_v, g_av, 1, 1)
        s_aa = g_aa - dot32(u_a, u_a, 0, 0)
        s_ad = g_ad - dot32(u_a, u_d, 0, 0)
        e_a = eliminate(s_aa, work)
        u_ad = dot32(e_a, s_ad, 1, 0)
        a_v = -dot32(e_a, dot32(u_a, e_v, 0, 0), 1, 0)
        d_v = d_e + dot32(u_ad, a_v, 0, 0)
        d_a = dot32(u_ad, e_a, 0, 0)
        c_v = v_e + dot32(rz_a, a_v, 0, 0)
        c_a = dot32(rz_a, e_a, 0, 0)
        e_d = eliminate(s_dd - dot32(u_ad, u_ad, 0, 0), work)
        c_d = dot32(rz_d, e_d, 0, 0)
        c_v = c_v - dot32(c_d, d_v, 1, 0)
        c_a = c_a - dot32(c_d, d_a, 1, 0)
        ch, cl = split(jnp.concatenate([c_v, c_d, c_a], axis=1))
        if it + 1 < ITERS:
            x = dot3(ch[0:K], cl[0:K], sh[...], sl[...], 1, 0)
            y = dot3(ch[K : 2 * K], cl[K : 2 * K], sh[...], sl[...], 1, 0)
            put_vectors(it + 1, x)
            fd[...] = y
        else:
            new = dot3(ch, cl, sh[...], sl[...], 1, 0)
            out[...] = new

    ref = tb.at[0, 0 : nz - 1]
    remote(ref, ref, tb_s.at[0], tb_r.at[0], sib).wait_send()
    remote(tb.at[c], tb.at[c], tbx_s.at[0], tbx_r.at[0], sib).wait_send()
    for it in range(ITERS):
        drain_exchange(it)
    for k in range(1 + ITERS):
        sum_drain(k)


def shards(ng, nr, sv, sd, tiles, tile_row, tile_slot, tile_count, send_row, send_grp, ritz):
    nz = nr // 2
    slots, width = tiles.shape[0], sv.shape[1]
    pos_a = near_positions(nz)
    far0 = pos_a * 2 * RB
    len_a = RB + 2 * (ng - 1) + 2 * (2 * pos_a - 1)
    len_b = 4 * (nz - pos_a)
    pieces = 12 if ng >= 12 else 3
    prow = 96 // pieces
    calls = 1 + ITERS
    dma = pltpu.SemaphoreType.DMA
    vmem, hbm = pl.BlockSpec(memory_space=pltpu.VMEM), pl.BlockSpec(memory_space=pl.ANY)
    both = pl.pallas_call(
        functools.partial(kernel, ng, nz, width * ng * nr, slots),
        out_shape=jax.ShapeDtypeStruct((2 * K, width), F32),
        in_specs=[hbm] * 9,
        out_specs=vmem,
        scratch_shapes=[
            pltpu.VMEM((ITERS, far0 + 2 * ng, K, BS), BF16),
            pltpu.VMEM((ITERS, (nz - pos_a) * 2 * RB, K, BS), BF16),
            pltpu.VMEM((ITERS, 2 * ng, K, BS), BF16),
            pltpu.VMEM((RB, K, BS), BF16),
            pltpu.VMEM(tiles.shape, BF16),
            pltpu.VMEM((len_a, K, BS), F32),
            pltpu.VMEM((len_b, K, BS), F32),
            pltpu.VMEM((3 * K, width), BF16),
            pltpu.VMEM((3 * K, width), BF16),
            pltpu.VMEM((K, width), F32),
            pltpu.VMEM(ritz.shape, F32),
            pltpu.VMEM((1, slots), I32),
            pltpu.VMEM((1, slots), I32),
            pltpu.VMEM((1, 4 * nz), I32),
            pltpu.VMEM((8, 128), I32),
            pltpu.VMEM((8, 128), I32),
            pltpu.SMEM((8, 128), I32),
            pltpu.SMEM((1,), I32),
            pltpu.SMEM(send_grp.shape, I32),
            pltpu.VMEM((8, 128), I32),
            pltpu.VMEM((2, nz, 8, 128), I32),
            pltpu.VMEM((128, 128), I32),
            pltpu.VMEM((calls, 96, 128), F32),
            pltpu.VMEM((calls, 2 * ng, prow, 128), F32),
            pltpu.VMEM((calls, nz, prow, 128), F32),
            pltpu.VMEM((calls, 96, 128), F32),
            pltpu.VMEM((K, 2 * K), F32),
            dma((11,)),
            dma((ITERS, 2)),
            dma((ITERS, 2, nz // 2, NCH)),
            dma((ITERS,)),
            dma((ITERS, 2)),
            dma((ITERS,)),
            dma((ITERS,)),
            dma((1,)),
            dma((1,)),
            dma((1,)),
            dma((1,)),
            dma((calls,)),
            dma((calls,)),
            dma((calls,)),
            dma((calls,)),
            dma((calls,)),
            dma((calls,)),
        ],
        compiler_params=pltpu.CompilerParams(
            collective_id=0, has_side_effects=True, vmem_limit_bytes=60 * 1024 * 1024
        ),
    )(
        sv, sd, tiles, tile_row.reshape(1, -1), tile_slot.reshape(1, -1), tile_count,
        send_row.reshape(1, -1), send_grp, ritz,
    )
    return both[:K], both[K:]


def solution(mesh):
    spread = P(None, ("grp", "row"))
    flat = P(("grp", "row"))
    return jax.shard_map(
        functools.partial(shards, mesh.shape["grp"], mesh.shape["row"]),
        mesh=mesh,
        in_specs=(spread, spread, P(("grp", "row"), None, None)) + (flat,) * 5 + (P(),),
        out_specs=(spread, spread),
        check_vma=False,
    )
```

```python
import functools

import jax
import jax.numpy as jnp
from jax import lax
from jax.experimental import pallas as pl
from jax.experimental.pallas import tpu as pltpu
from jax.sharding import PartitionSpec as P

ITERS = 2
K = 64
BS = 128
RB = 8
NCH = 4
BPC = RB // NCH
F32, BF16, I32 = jnp.float32, jnp.bfloat16, jnp.int32
MESH = pl.DeviceIdType.MESH
HIGH = lax.Precision.HIGHEST


def dot32(a, b, ca, cb):
    return lax.dot_general(
        a, b, (((ca,), (cb,)), ((), ())), precision=HIGH, preferred_element_type=F32
    )


def dot16(a, b, ca, cb):
    return lax.dot_general(a, b, (((ca,), (cb,)), ((), ())), preferred_element_type=F32)


def split(x):
    hi = x.astype(BF16)
    return hi, (x - hi.astype(F32)).astype(BF16)


def dot3(ah, al, bh, bl, ca, cb):
    return dot16(ah, bh, ca, cb) + (dot16(ah, bl, ca, cb) + dot16(al, bh, ca, cb))


class Eliminate:
    def __init__(self, s, work):
        row = lax.broadcasted_iota(I32, (K, K), 0)
        col = lax.broadcasted_iota(I32, (K, K), 1)
        work[:, 0:K] = s
        work[:, K : 2 * K] = jnp.where(row == col, 1.0, 0.0).astype(F32)
        self.rows = [work[8 * i : 8 * i + 8, :] for i in range(K // 8)]
        self.sub = lax.broadcasted_iota(I32, (8, 2 * K), 0)

    def panel(self, p):
        rows, sub = self.rows, self.sub
        wide = (8, 2 * K)
        cols = [
            [
                jnp.broadcast_to(rows[i][:, 8 * p + k : 8 * p + k + 1], wide)
                for i in range(p, K // 8)
            ]
            for k in range(8)
        ]
        for k in range(8):
            inv = lax.rsqrt(jnp.broadcast_to(cols[k][0][k : k + 1, :], wide))
            low = [c * inv for c in cols[k]]
            for j in range(k + 1, 8):
                mult = jnp.broadcast_to(low[0][j : j + 1, :], wide)
                cols[j] = [c - x * mult for c, x in zip(cols[j], low)]
            pivot = jnp.broadcast_to(rows[p][k : k + 1, :], wide) * inv
            below = jnp.where(sub > k, low[0], 0.0)
            rows[p] = jnp.where(sub == k, pivot, rows[p] - below * pivot)
            for i in range(p + 1, K // 8):
                rows[i] = rows[i] - low[i - p] * pivot

    def inverse(self):
        return jnp.concatenate([r[:, K : 2 * K] for r in self.rows], axis=0)


def eliminate(s, work):
    elim = Eliminate(s, work)
    for p in range(K // 8):
        elim.panel(p)
    return elim.inverse()


def tree_sum(xs):
    while len(xs) > 1:
        xs = [a + b for a, b in zip(xs[0::2], xs[1::2])] + ([xs[-1]] if len(xs) % 2 else [])
    return xs[0]


def near_positions(nz):
    return 2 * (nz // 2 * 5 // 8) + 1


def kernel(
    ng, nz, total_rows, slots,
    sv, sd, tiles, tile_row, tile_slot, count, send_row, send_grp, ritz,
    out,
    blk_a, blk_b, pack, own, tl, runs_a, runs_b, sh, sl, fd, rz, row_in, slot_in, row_list, iv, ov, sm_iv, sm_count, sm_far,
    mytb, tb, tv, pay, rsb, zb, res, work,
    loc_sem, ring_s, ring_r, sib_s, sib_r, far_s, far_r, tb_s, tb_r, tbx_s, tbx_r,
    rs_s, rs_r, z_s, z_r, ag_s, ag_r,
):
    hops, pos_a = nz // 2, near_positions(nz)
    far0 = pos_a * 2 * RB
    rows_a, rows_b = far0 + 2 * ng, (nz - pos_a) * 2 * RB
    len_a, len_b = runs_a.shape[0], runs_b.shape[0]
    pieces = 12 if ng >= 12 else 3
    prow = 96 // pieces
    side = round(ng**0.5)
    g, r = lax.axis_index("grp"), lax.axis_index("row")
    z, c = r // 2, r % 2
    gx, gy = g // side, g % side
    m = g * 2 + c
    sib = (g, z * 2 + (1 - c))

    def remote(src, dst, ss, rs, dev):
        return pltpu.make_async_remote_copy(
            src_ref=src, dst_ref=dst, send_sem=ss, recv_sem=rs, device_id=dev, device_id_type=MESH
        )

    def wrap(i, n):
        return jnp.where(i >= n, i - n, i)

    z_steps = sorted(range(1, nz), key=lambda k: -min(k, nz - k))
    plane_steps = sorted(
        [(i, j, k) for i in range(side) for j in range(side) for k in range(2) if (i, j, k) != (0, 0, 0)],
        key=lambda t: -min(t[0], side - t[0]) - min(t[1], side - t[1]),
    )

    def z_dev(k):
        return (g, wrap(z + k, nz) * 2 + c)

    def plane_dev(t):
        core = 1 - c if t[2] else c
        return (wrap(gx + t[0], side) * side + wrap(gy + t[1], side), z * 2 + core)

    loads = [
        pltpu.make_async_copy(src, dst, loc_sem.at[i])
        for i, (src, dst) in enumerate(
            [(sv, out.at[0:K]), (sd, fd), (tiles, tl), (tile_row, row_in), (tile_slot, slot_in),
             (send_row, row_list), (send_grp, sm_far), (ritz, rz), (count, sm_count)]
        )
    ]
    for cp in loads:
        cp.start()

    barrier = pltpu.get_barrier_semaphore()
    for k in z_steps:
        pl.semaphore_signal(barrier, inc=1, device_id=z_dev(k), device_id_type=MESH)
    for t in plane_steps:
        pl.semaphore_signal(barrier, inc=1, device_id=plane_dev(t), device_id_type=MESH)

    def place(d, hop):
        if hop == 0:
            return 0
        return nz - 1 if hop == hops else 2 * hop - 1 + d

    def chunk(it, pos, core, j=0, n=RB):
        if pos < pos_a:
            return blk_a.at[it, pl.ds(pos * 2 * RB + core * RB + j * BPC, n)]
        return blk_b.at[it, pl.ds((pos - pos_a) * 2 * RB + core * RB + j * BPC, n)]

    def ring_copy(it, d, hop, j):
        to = z_dev(1) if d == 0 else z_dev(nz - 1)
        return remote(
            chunk(it, place(d, hop - 1), c, j, BPC), chunk(it, place(d, hop), c, j, BPC),
            ring_s.at[it, d], ring_r.at[it, d, hop - 1, j], to,
        )

    def ring_here(it, d, hop, j):
        ref = chunk(it, place(d, hop), c, j, BPC)
        return remote(ref, ref, ring_s.at[it, d], ring_r.at[it, d, hop - 1, j], sib)

    def sib_copy(it, d, hop):
        pos = place(d, hop)
        half = hop == hops
        ref = chunk(it, pos, c, NCH // 2 if half and d else 0, RB // 2 if half else RB)
        return remote(ref, ref, sib_s.at[it], sib_r.at[it, int(pos >= pos_a)], sib)

    def ring_has(d, hop, j):
        return hop < hops or (hop == hops and (j < NCH // 2) == (d == 0))

    def far_copy(it, t):
        dev = plane_dev(t)
        return remote(
            pack.at[it, pl.ds(dev[0] * 2, 2)], blk_a.at[it, pl.ds(far0 + 2 * g, 2)],
            far_s.at[it], far_r.at[it], dev,
        )

    far_steps = [t for t in plane_steps if t[2] == 0]

    def drain_exchange(it):
        a, n = blk_a.at[it, pl.ds(0, nz * RB)], (hops - 1) * RB + RB // 2
        remote(a, a, sib_s.at[it], sib_r.at[it, 0], sib).wait_send()
        part = blk_a.at[it, pl.ds(0, n)]
        for d in range(2):
            remote(part, part, ring_s.at[it, d], ring_r.at[it, d, 0, 0], sib).wait_send()
        part = pack.at[it, pl.ds(0, 2 * ng - 2)]
        remote(part, part, far_s.at[it], far_r.at[it], sib).wait_send()

    mine = pl.ds(pl.multiple_of(lax.rem(g, pieces) * prow, 8), prow)

    def owner_core(k, j):
        return (j + (k == 0)) % 2

    def owner(k):
        return (g < pieces) & (c == lax.rem(g + (k == 0), 2))

    def is_mine(k, j):
        return (g == j) & (c == owner_core(k, j))

    def either(k, yes, no):
        @pl.when(owner(k))
        def _():
            yes()

        @pl.when(jnp.logical_not(owner(k)))
        def _():
            no()

    def sum_start(k):
        for j in range(pieces):
            ref = pay.at[k, j * prow : (j + 1) * prow]

            @pl.when(is_mine(k, j))
            def _():
                rsb[k, m] = ref[...]

            @pl.when(jnp.logical_not(is_mine(k, j)))
            def _():
                remote(ref, rsb.at[k, m], rs_s.at[k], rs_r.at[k], (j, z * 2 + owner_core(k, j))).start()

    def sum_plane(k):
        @pl.when(owner(k))
        def _():
            ref = rsb.at[k, 0 : 2 * ng - 1]
            remote(ref, ref, rs_s.at[k], rs_r.at[k], sib).wait_recv()
            zb[k, z] = tree_sum([rsb[k, i] for i in range(2 * ng)])
            for s in z_steps:
                remote(zb.at[k, z], zb.at[k, z], z_s.at[k], z_r.at[k], z_dev(s)).start()

    def sum_z(k):
        @pl.when(owner(k))
        def _():
            ref = zb.at[k, 0 : nz - 1]
            remote(ref, ref, z_s.at[k], z_r.at[k], sib).wait_recv()
            res[k, mine] = tree_sum([zb[k, i] for i in range(nz)])
            for t in plane_steps:
                remote(res.at[k, mine], res.at[k, mine], ag_s.at[k], ag_r.at[k], plane_dev(t)).start()

    def sum_end(k):
        def wait(n):
            ref = res.at[k, 0 : n * prow]
            remote(ref, ref, ag_s.at[k], ag_r.at[k], sib).wait_recv()

        either(k, lambda: wait(pieces - 1), lambda: wait(pieces))

    def sum_drain(k):
        def wait(ref, sem):
            remote(ref, ref, sem, ag_r.at[k], sib).wait_send()

        def yes():
            wait(pay.at[k, 0 : (pieces - 1) * prow], rs_s.at[k])
            wait(zb.at[k, 0 : nz - 1], z_s.at[k])
            wait(rsb.at[k, 0 : 2 * ng - 1], ag_s.at[k])

        either(k, yes, lambda: wait(pay.at[k], rs_s.at[k]))

    def put_sums(k, wide, square):
        pay[k, 0:K, :] = wide
        pay[k, K : K + K // 2, 0:K] = square[0 : K // 2]
        pay[k, K : K + K // 2, K : 2 * K] = square[K // 2 : K]

    def get_sums(k):
        scale = 1.0 / total_rows
        left = res[k, 0:K, 0:K] * scale
        right = res[k, 0:K, K : 2 * K] * scale
        square = jnp.concatenate(
            [res[k, K : K + K // 2, 0:K], res[k, K : K + K // 2, K : 2 * K]], axis=0
        )
        return left, right, square * scale

    def order_tiles():
        for i in (3, 4, 8):
            loads[i].wait()
        iv[...] = jnp.zeros((8, 128), I32)
        iv[0:1, 0:slots] = row_in[...]
        iv[1:2, 0:slots] = slot_in[...]
        lane = lax.broadcasted_iota(I32, (128, 128), 1)
        subl = lax.broadcasted_iota(I32, (128, 128), 0)
        row_r = jnp.broadcast_to(iv[0:1, :], (128, 128))
        slot_r = jnp.broadcast_to(iv[1:2, :], (128, 128))
        step = lax.shift_right_arithmetic(slot_r - RB, 2) - z
        step = jnp.where(step < 0, step + nz, step)
        late = (slot_r >= RB) & (slot_r < RB + 4 * nz)
        late = late & (jnp.minimum(step, nz - step) * 2 >= pos_a)
        key_r = jnp.where(late, 1024, 0) + row_r * 128 + lane
        key_r = jnp.where(lane < sm_count[0], key_r, 4096 + lane)
        row_c, slot_c, key_c = row_r.T, slot_r.T, key_r.T
        rank_r = jnp.sum(jnp.where(key_c < key_r, 1, 0), axis=0, keepdims=True)
        hit = jnp.broadcast_to(rank_r, (128, 128)).T == lane

        def total(x):
            return jnp.sum(x, axis=0, keepdims=True)

        ov[...] = jnp.zeros((8, 128), I32)
        ov[0:1, :] = total(jnp.where(hit, subl, 0))
        ov[1:2, :] = total(jnp.where(hit, slot_c, 0))
        ov[2:3, :] = total(jnp.where(hit, row_c, 0))
        ov[3:4, :] = total(jnp.where((key_c < 1024) & (row_c <= lane), 1, 0))
        ov[4:5, :] = total(jnp.where((key_c >= 1024) & (key_c < 4096) & (row_c <= lane), 1, 0))

    def send_table():
        loads[5].wait()
        mytb[...] = jnp.zeros((8, 128), I32)
        mytb[0:1, 0 : 4 * nz] = row_list[...]
        tb[c, z] = mytb[...]
        for k in z_steps:
            remote(mytb, tb.at[c, z], tb_s.at[0], tb_r.at[0], z_dev(k)).start()

    def pass_table():
        ref = tb.at[0, 0 : nz - 1]
        remote(ref, ref, tb_s.at[0], tb_r.at[0], sib).wait_recv()
        remote(tb.at[c], tb.at[c], tbx_s.at[0], tbx_r.at[0], sib).start()

    def take_table():
        remote(tb.at[1 - c], tb.at[1 - c], tbx_s.at[0], tbx_r.at[0], sib).wait_recv()
        tv[...] = jnp.zeros((128, 128), I32)
        for i in range(2 * nz):
            tv[i : i + 1, :] = tb[i % 2, i // 2, 0:1, :]
        tv[...] = tv[...].T

    def index_tiles():
        def column(s):
            return jnp.broadcast_to(tv[pl.ds(2 * r + s, 1), :], (128, 128)).T

        sender = lax.broadcasted_iota(I32, (128, 128), 0)
        e = ov[1:2, :]
        p = lax.shift_right_arithmetic(e - RB, 1)
        listed = jnp.where(jnp.broadcast_to(e & 1, (128, 128)) == 0, column(0), column(1))
        q = jnp.sum(jnp.where(sender == jnp.broadcast_to(p, (128, 128)), listed, 0), axis=0, keepdims=True)
        away = lax.shift_right_arithmetic(p, 1) - z
        away = jnp.where(away < 0, away + nz, away)
        pos = jnp.where(away < hops, 2 * away, 2 * (nz - away) - 1)
        pos = jnp.where(pos >= pos_a, pos - pos_a, pos)
        near = pos * 2 * RB + (p & 1) * RB + q
        far = far0 + e - RB - 4 * nz
        ov[5:6, :] = jnp.where(e < RB, c * RB + e, jnp.where(e < RB + 4 * nz, near, far))
        pltpu.make_async_copy(ov, sm_iv, loc_sem.at[9]).start()

    def read_table():
        pltpu.make_async_copy(ov, sm_iv, loc_sem.at[9]).wait()

    def tile_step(acc, block, i, fresh):
        product = dot16(block, tl[jnp.clip(sm_iv[0, i], 0, slots - 1)], 1, 1)
        if fresh:
            return product
        keep = jnp.where(sm_iv[2, i] == sm_iv[2, i - 1], 1.0, 0.0).astype(F32)
        return acc * keep + product

    def tiles_early(it, state, first, last):
        acc = state.get("acc")
        for i in range(first, min(last, len_a)):
            acc = tile_step(acc, blk_a[it, jnp.clip(sm_iv[5, i], 0, rows_a - 1)], i, i == 0)
            runs_a[i] = acc
        state["acc"] = acc

    def tiles_late(it):
        first, acc = jnp.clip(sm_iv[3, RB - 1], 0, len_a), None
        for u in range(len_b):
            i = first + u
            acc = tile_step(acc, blk_b[it, jnp.clip(sm_iv[5, i], 0, rows_b - 1)], i, u == 0)
            runs_b[u] = acc
        for b in range(RB):
            x = 0.0
            for line, runs, size in ((3, runs_a, len_a), (4, runs_b, len_b)):
                end = sm_iv[line, b]
                before = sm_iv[line, b - 1] if b else jnp.int32(0)
                some = jnp.where(end > before, 1.0, 0.0).astype(F32)
                x = x + runs[jnp.clip(end - 1, 0, size - 1)] * some
            hi, lo = split(x)
            sh[2 * K : 3 * K, b * BS : (b + 1) * BS] = hi
            sl[2 * K : 3 * K, b * BS : (b + 1) * BS] = lo

    def split_into(row0, x):
        hi, lo = split(x)
        sh[row0 : row0 + K, :] = hi
        sl[row0 : row0 + K, :] = lo

    def put_vectors(it, x):
        split_into(0, x)
        for b in range(RB):
            part = sh[0:K, b * BS : (b + 1) * BS]
            own[b] = part
            blk_a[it, c * RB + b] = part

    def send_far(it):
        if it == 0:
            loads[6].wait()
        for h in range(ng):
            for s in range(2):
                pack[it, h * 2 + s] = own[jnp.clip(sm_far[h * 2 + s], 0, RB - 1)]
        zero = jnp.zeros((K, BS), BF16)
        blk_a[it, far0 + 2 * g] = zero
        blk_a[it, far0 + 2 * g + 1] = zero
        for t in far_steps:
            far_copy(it, t).start()

    def wait_early(it):
        ref = blk_a.at[it, pl.ds(0, pos_a * RB)]
        remote(ref, ref, sib_s.at[it], sib_r.at[it, 0], sib).wait_recv()
        ref = blk_a.at[it, pl.ds(0, 2 * ng - 2)]
        remote(ref, ref, far_s.at[it], far_r.at[it], sib).wait_recv()

    def wait_late(it):
        ref = blk_b.at[it, pl.ds(0, (nz - pos_a) * RB)]
        remote(ref, ref, sib_s.at[it], sib_r.at[it, 1], sib).wait_recv()

    def first_products():
        put_sums(
            0,
            dot3(sh[0:K], sl[0:K], sh[0 : 2 * K], sl[0 : 2 * K], 1, 1),
            dot3(sh[K : 2 * K], sl[K : 2 * K], sh[K : 2 * K], sl[K : 2 * K], 1, 1),
        )

    def get_directions(it):
        if it == 0:
            loads[1].wait()
        split_into(K, fd[...])

    loads[0].wait()
    put_vectors(0, out[0:K])
    pl.semaphore_wait(barrier, nz - 1 + 2 * ng - 1)

    for it in range(ITERS):
        k0, k1 = 0, 1 + it
        for j in range(NCH):
            for d in range(2):
                ring_copy(it, d, 1, j).start()
        sib_copy(it, 0, 0).start()

        state = {}
        early = hops * 5 // 8 * NCH + 1
        ready = early - max(1, NCH // 2)
        last = (hops - 1) * NCH + NCH // 2
        send_far(it)
        get_directions(it)
        plan = []
        if it == 0:
            mid = ready // 2 + 1
            tail = max(mid + 2, ready - 4)
            send_table()
            first_products()
            order_tiles()
            plan += [
                (1, functools.partial(sum_start, k0)),
                (mid, functools.partial(sum_plane, k0)),
                (mid + 1, pass_table),
                (tail, take_table),
                (tail + 1, index_tiles),
                (tail + 3, read_table),
            ]
            early = max(early, tail + 4)
        plan += [(early, functools.partial(wait_early, it))]
        if it == 0:
            plan += [(early, lambda: loads[2].wait())]
        part = -(-len_a // max(1, last - early))
        for i in range(-(-len_a // part)):
            plan += [(early + i, functools.partial(tiles_early, it, state, i * part, (i + 1) * part))]
        plan = sorted(enumerate(plan), key=lambda t: (t[1][0], t[0]))
        plan = [t[1] for t in plan]

        step = 0
        for hop in range(1, hops + 1):
            for j in range(NCH):
                for d in range(2):
                    if ring_has(d, hop, j):
                        ring_here(it, d, hop, j).wait_recv()
                        if ring_has(d, hop + 1, j):
                            ring_copy(it, d, hop + 1, j).start()
                        if not ring_has(d, hop, j + 1) or j == NCH - 1:
                            sib_copy(it, d, hop).start()
                while plan and plan[0][0] <= step:
                    plan.pop(0)[1]()
                step += 1
        for _, work_left in plan:
            work_left()
        wait_late(it)
        tiles_late(it)
        put_sums(
            k1,
            dot3(sh[2 * K : 3 * K], sl[2 * K : 3 * K], sh[0 : 2 * K], sl[0 : 2 * K], 1, 1),
            dot3(sh[2 * K : 3 * K], sl[2 * K : 3 * K], sh[2 * K : 3 * K], sl[2 * K : 3 * K], 1, 1),
        )
        sum_start(k1)
        if it == 0:
            loads[7].wait()
            sum_z(k0)
            sum_plane(k1)
            sum_end(k0)
            g_vv, g_vd, g_dd = get_sums(k0)
        else:
            before = rz[it - 1]
            wide = dot32(before, before, 0, 0)
            g_vv, g_vd, g_dd = wide[0:K, 0:K], wide[0:K, K : 2 * K], wide[K : 2 * K, K : 2 * K]
        rz_v, rz_a, rz_d = (rz[it, i * K : (i + 1) * K, :] for i in range(3))
        e_v = eliminate(g_vv, work)
        u_d = dot32(e_v, g_vd, 1, 0)
        s_dd = g_dd - dot32(u_d, u_d, 0, 0)
        if it:
            sum_plane(k1)
        d_e = dot32(u_d, e_v, 0, 0)
        v_e = dot32(rz_v, e_v, 0, 0)
        sum_z(k1)
        sum_end(k1)
        g_av, g_ad, g_aa = get_sums(k1)
        u_a = dot32(e_v, g_av, 1, 1)
        s_aa = g_aa - dot32(u_a, u_a, 0, 0)
        s_ad = g_ad - dot32(u_a, u_d, 0, 0)
        e_a = eliminate(s_aa, work)
        u_ad = dot32(e_a, s_ad, 1, 0)
        a_v = -dot32(e_a, dot32(u_a, e_v, 0, 0), 1, 0)
        d_v = d_e + dot32(u_ad, a_v, 0, 0)
        d_a = dot32(u_ad, e_a, 0, 0)
        c_v = v_e + dot32(rz_a, a_v, 0, 0)
        c_a = dot32(rz_a, e_a, 0, 0)
        e_d = eliminate(s_dd - dot32(u_ad, u_ad, 0, 0), work)
        c_d = dot32(rz_d, e_d, 0, 0)
        c_v = c_v - dot32(c_d, d_v, 1, 0)
        c_a = c_a - dot32(c_d, d_a, 1, 0)
        ch, cl = split(jnp.concatenate([c_v, c_d, c_a], axis=1))
        if it + 1 < ITERS:
            x = dot3(ch[0:K], cl[0:K], sh[...], sl[...], 1, 0)
            y = dot3(ch[K : 2 * K], cl[K : 2 * K], sh[...], sl[...], 1, 0)
            put_vectors(it + 1, x)
            fd[...] = y
        else:
            new = dot3(ch, cl, sh[...], sl[...], 1, 0)
            out[...] = new

    ref = tb.at[0, 0 : nz - 1]
    remote(ref, ref, tb_s.at[0], tb_r.at[0], sib).wait_send()
    remote(tb.at[c], tb.at[c], tbx_s.at[0], tbx_r.at[0], sib).wait_send()
    for it in range(ITERS):
        drain_exchange(it)
    for k in range(1 + ITERS):
        sum_drain(k)


def shards(ng, nr, sv, sd, tiles, tile_row, tile_slot, tile_count, send_row, send_grp, ritz):
    nz = nr // 2
    slots, width = tiles.shape[0], sv.shape[1]
    pos_a = near_positions(nz)
    far0 = pos_a * 2 * RB
    len_a = RB + 2 * (ng - 1) + 2 * (2 * pos_a - 1)
    len_b = 4 * (nz - pos_a)
    pieces = 12 if ng >= 12 else 3
    prow = 96 // pieces
    calls = 1 + ITERS
    dma = pltpu.SemaphoreType.DMA
    vmem, hbm = pl.BlockSpec(memory_space=pltpu.VMEM), pl.BlockSpec(memory_space=pl.ANY)
    both = pl.pallas_call(
        functools.partial(kernel, ng, nz, width * ng * nr, slots),
        out_shape=jax.ShapeDtypeStruct((2 * K, width), F32),
        in_specs=[hbm] * 9,
        out_specs=vmem,
        scratch_shapes=[
            pltpu.VMEM((ITERS, far0 + 2 * ng, K, BS), BF16),
            pltpu.VMEM((ITERS, (nz - pos_a) * 2 * RB, K, BS), BF16),
            pltpu.VMEM((ITERS, 2 * ng, K, BS), BF16),
            pltpu.VMEM((RB, K, BS), BF16),
            pltpu.VMEM(tiles.shape, BF16),
            pltpu.VMEM((len_a, K, BS), F32),
            pltpu.VMEM((len_b, K, BS), F32),
            pltpu.VMEM((3 * K, width), BF16),
            pltpu.VMEM((3 * K, width), BF16),
            pltpu.VMEM((K, width), F32),
            pltpu.VMEM(ritz.shape, F32),
            pltpu.VMEM((1, slots), I32),
            pltpu.VMEM((1, slots), I32),
            pltpu.VMEM((1, 4 * nz), I32),
            pltpu.VMEM((8, 128), I32),
            pltpu.VMEM((8, 128), I32),
            pltpu.SMEM((8, 128), I32),
            pltpu.SMEM((1,), I32),
            pltpu.SMEM(send_grp.shape, I32),
            pltpu.VMEM((8, 128), I32),
            pltpu.VMEM((2, nz, 8, 128), I32),
            pltpu.VMEM((128, 128), I32),
            pltpu.VMEM((calls, 96, 128), F32),
            pltpu.VMEM((calls, 2 * ng, prow, 128), F32),
            pltpu.VMEM((calls, nz, prow, 128), F32),
            pltpu.VMEM((calls, 96, 128), F32),
            pltpu.VMEM((K, 2 * K), F32),
            dma((11,)),
            dma((ITERS, 2)),
            dma((ITERS, 2, nz // 2, NCH)),
            dma((ITERS,)),
            dma((ITERS, 2)),
            dma((ITERS,)),
            dma((ITERS,)),
            dma((1,)),
            dma((1,)),
            dma((1,)),
            dma((1,)),
            dma((calls,)),
            dma((calls,)),
            dma((calls,)),
            dma((calls,)),
            dma((calls,)),
            dma((calls,)),
        ],
        compiler_params=pltpu.CompilerParams(
            collective_id=0, has_side_effects=True, vmem_limit_bytes=60 * 1024 * 1024
        ),
    )(
        sv, sd, tiles, tile_row.reshape(1, -1), tile_slot.reshape(1, -1), tile_count,
        send_row.reshape(1, -1), send_grp, ritz,
    )
    return both[:K], both[K:]


def solution(mesh):
    spread = P(None, ("grp", "row"))
    flat = P(("grp", "row"))
    return jax.shard_map(
        functools.partial(shards, mesh.shape["grp"], mesh.shape["row"]),
        mesh=mesh,
        in_specs=(spread, spread, P(("grp", "row"), None, None)) + (flat,) * 5 + (P(),),
        out_specs=(spread, spread),
        check_vma=False,
    )
```
